32 devices in a mesh: row: 8 (over z, y), col: 4 (over x, core).
Axes of the slice: x: 2, y: 2, z: 4, core: 2. Of those that a mesh axis runs over, the one named last changes fastest.
Arguments:
- a_tiles: bfloat16 [128, 27, 128, 128], P('row'), may hold values from -0.109375 to 0.109375
- a_cols: int32 [128, 27], P('row'), may hold values from 0 to 19, as said below
- p_tiles: bfloat16 [128, 4, 128, 128], P('row', 'col'), may hold values from -2 to 2
- p_cols: int32 [128, 4], P('row', 'col'), may hold values from 0 to 15, as said below
- send_rows: int32 [16, 2], P('row'), may hold values from 0 to 15, as said below
Outputs:
- coarse_matrix: float32 [16, 16, 128, 128], P('row', 'col')
The draws below stay inside these ranges and needn't reach their ends.
Inputs may be any that keep to these rules, and one draw needn't show every extreme that they name: `a_cols`: an entry below 16 names a fine block row of the device's own slab; an entry 16 + t with t < 2 names the t-th row that the previous slab sends to this slab, and 18 + t the t-th row that the next slab sends to it. Every slab reads all 4 rows that it receives. Slabs are periodic. `p_cols`: the coarse block column of slot k in fine block row i is congruent to k modulo 4 and lies among the 6 consecutive ids that start at ((i div 16) - 1) * 2, modulo 16. `send_rows`: each row lists 2 distinct slab-local rows.
All inputs are finite; a program needn't handle non-finite values.
Results may differ from the reference program's by a relative error of at most 0.0029.
Values may be sent and summed in bfloat16 or wider, within the bound.
A program may use at most 192 MiB of HBM per device.

```python
import jax
import jax.numpy as jnp
from jax import lax

TILE = 128
KA = 27
BR = 16
CB = 2
CAPF = 2
KP = 4
NB = 128
NC = 16
NCC = 4
N_ROW = 8
N_COL = 4


def draw_a_cols(key, part):
    key = jax.random.fold_in(key, 11)
    keys = jax.random.split(key, 3)
    own_refs = jax.random.randint(keys[0], (N_ROW, BR, KA), 0, BR)
    ghost_refs = BR + jax.random.randint(keys[1], (N_ROW, BR, KA), 0, 2 * CAPF)
    selector = jax.random.randint(keys[2], (N_ROW, BR, KA), 0, 3)
    references = jnp.where(selector == 0, ghost_refs, own_refs)
    forced = BR + jnp.arange(2 * CAPF)
    references = references.at[:, BR - 1, 1:1 + 2 * CAPF].set(forced[None, :])
    references = references.at[:, 0, 0].set(0)
    return references.reshape(N_ROW * BR, KA).astype(jnp.int32)


def draw_p_cols(key, part):
    key = jax.random.fold_in(key, 13)
    fine_rows = jnp.arange(NB)
    slab_ids = fine_rows // BR
    slot_ids = jnp.arange(KP)
    window_base = (slab_ids - 1) * CB
    offsets = jnp.mod(slot_ids[None, :] - window_base[:, None], N_COL)
    option_count = (3 * CB - 1 - offsets) // N_COL + 1
    picks = jax.random.randint(key, (NB, KP), 0, 1 << 20) % option_count
    picks = jnp.where((fine_rows % BR == 0)[:, None], 0, picks)
    coarse_ids = jnp.mod(window_base[:, None] + offsets + N_COL * picks, NC)
    return coarse_ids.astype(jnp.int32)


def draw_send_rows(key, part):
    key = jax.random.fold_in(key, 12)
    scores = jax.random.randint(key, (2 * N_ROW, BR), 0, 1 << 20)
    chosen = jnp.argsort(scores, axis=1, stable=True)[:, :CAPF]
    first_list = jnp.concatenate([jnp.array([BR - 1]), jnp.arange(CAPF - 1)])
    chosen = chosen.at[0].set(first_list)
    return chosen.astype(jnp.int32)


def steps_of(key, dims, cuts, least, high):
    def one(axis_at, shards_of):
        draws = jax.random.uniform(jax.random.fold_in(jax.random.fold_in(key, 6), axis_at), (shards_of,), jnp.float32, least / len(cuts), high / len(cuts))
        return jnp.repeat(jnp.exp(draws), dims[axis_at] // shards_of).reshape((-1,) + (1,) * (len(dims) - axis_at - 1))

    loudness = one(*cuts[0])
    for cut in cuts[1:]:
        loudness = loudness * one(*cut)
    return loudness


def centred(stream_key, dims, width, reach, pieces=(), kind=jnp.bfloat16):
    factor_of = steps_of(stream_key, dims, pieces, -0.22, 0.18) if pieces else 1.0
    values = jax.random.normal(stream_key, dims, jnp.float32) * width * factor_of
    return jnp.minimum(jnp.maximum(values, -reach), reach).astype(kind)


def setup_inputs(seed: int = 0) -> dict:
    key_list = jax.random.split(jax.random.key(seed), 6)
    a_tiles = centred(key_list[0], (NB, KA, TILE, TILE), (KA * TILE) ** -0.5, 0.109375, ((0, 8),))
    a_cols = draw_a_cols(jax.random.fold_in(key_list[5], 71), 0)
    p_tiles = centred(key_list[2], (NB, KP, TILE, TILE), (max(TILE // 16, 1)) ** -0.5, 2.0, ((0, 8), (1, 4)))
    p_cols = draw_p_cols(jax.random.fold_in(key_list[5], 71), 0)
    send_rows = draw_send_rows(jax.random.fold_in(key_list[5], 71), 0)
    return {"a_tiles": a_tiles, "a_cols": a_cols, "p_tiles": p_tiles, "p_cols": p_cols, "send_rows": send_rows}


def reference(a_tiles, a_cols, p_tiles, p_cols, send_rows):
    def slab_step(coarse_sum, slab_index):
        first_row = slab_index * BR
        a_block = lax.dynamic_slice_in_dim(a_tiles, first_row, BR, 0).astype(jnp.float32)
        entries = lax.dynamic_slice_in_dim(a_cols, first_row, BR, 0)
        ghost_slot = jnp.clip(entries - BR, 0, 2 * CAPF - 1)
        side = ghost_slot // CAPF
        slot_number = ghost_slot % CAPF
        neighbour = jnp.mod(slab_index + 2 * side - 1, N_ROW).astype(jnp.int32)
        remote = neighbour * BR + send_rows[2 * neighbour + side, slot_number]
        fine_column = jnp.where(entries < BR, first_row + entries, remote).astype(jnp.int32)
        right_tiles = p_tiles[fine_column].astype(jnp.float32)
        right_ids = p_cols[fine_column]
        products = jnp.einsum('imxy,imlyz->imlxz', a_block, right_tiles,
                              precision=lax.Precision.HIGHEST).astype(jnp.bfloat16)
        left_tiles = lax.dynamic_slice_in_dim(p_tiles, first_row, BR, 0).astype(jnp.float32)
        left_ids = lax.dynamic_slice_in_dim(p_cols, first_row, BR, 0)
        tile_terms = jnp.einsum('ikyx,imlyz->ikmlxz', left_tiles, products.astype(jnp.float32),
                                precision=lax.Precision.HIGHEST)
        row_ids = jnp.broadcast_to(left_ids[:, :, None, None], tile_terms.shape[:4])
        column_ids = (right_ids % N_COL) * NCC + right_ids // N_COL
        column_ids = jnp.broadcast_to(column_ids[:, None, :, :], tile_terms.shape[:4])
        return coarse_sum.at[row_ids, column_ids].add(tile_terms), None

    zero_matrix = jnp.zeros((NC, NC, TILE, TILE), jnp.float32)
    result, unused = lax.scan(slab_step, zero_matrix, jnp.arange(N_ROW, dtype=jnp.int32))
    return result
```

```python
import functools

import jax
import jax.numpy as jnp
from jax import lax
from jax.experimental import pallas as pl
from jax.experimental.pallas import tpu as pltpu
from jax.sharding import PartitionSpec as P

CB = 2
SPAN = 3
PARTS = 4
MESH = pl.DeviceIdType.MESH


def wrap(value, size):
    return jnp.where(value < 0, value + size, value)


def kernel(
    rows,
    a_cols,
    p_cols,
    send_rows,
    p_ref,
    a_ref,
    out_ref,
    a_buf,
    ghost_out,
    ghost_out_ids,
    ghost_in,
    ghost_in_ids,
    slots,
    marks,
    right,
    grouped,
    part_out,
    part_in,
    a_sem,
    ghost_send,
    ghost_recv,
    slot_send,
    slot_recv,
    mark_send,
    mark_recv,
    part_send,
    part_recv,
):
    height, entries, tile = a_buf.shape[0], a_buf.shape[1], a_buf.shape[2]
    capacity = ghost_out.shape[1]
    coarse = CB * rows
    column_count = out_ref.shape[1]
    per_part = height // PARTS
    s = lax.axis_index("row")
    k = lax.axis_index("col")
    after, before = lax.rem(s + 1, rows), lax.rem(s + rows - 1, rows)
    mate = k + 1 - 2 * lax.rem(k, 2)
    across = lax.rem(k + 2, 4)
    facing = 3 - k

    def a_copy(i):
        return pltpu.make_async_copy(a_ref.at[i], a_buf.at[i], a_sem.at[i])

    for i in range(height):
        a_copy(i).start()

    barrier = pltpu.get_barrier_semaphore()
    for device in ({"row": before}, {"row": after}, {"col": mate}, {"col": across}):
        pl.semaphore_signal(barrier, inc=1, device_id=device, device_id_type=MESH)

    def first_id(slab):
        return lax.rem(CB * slab + coarse - 4, coarse)

    def first_column(slab):
        start = first_id(slab)
        offset = lax.rem(k + 4 - lax.rem(start, 4), 4)
        return lax.rem((start + offset) // 4, column_count)

    start = first_id(s)
    left_start = lax.rem(CB * s + coarse - 2, coarse)

    for side in range(2):
        for t in range(capacity):
            row = send_rows[side, t]
            ghost_out[side, t] = p_ref[row, 0]
            ghost_out_ids[side, t : t + 1] = jnp.full((1, tile), p_cols[row, 0], jnp.int32)
    for i in range(height):
        slots[0, i // per_part, :, (i % per_part) * tile : (i % per_part + 1) * tile] = p_ref[i, 0].T
        place = wrap(p_cols[i, 0] - left_start, coarse)
        marks[0, i : i + 1] = jnp.full((1, tile), jnp.where(place >= 4, 1.0, 0.0), jnp.float32)

    pl.semaphore_wait(barrier, 4)

    def ghost_copies(side):
        target = {"row": after if side == 0 else before}
        return [
            pltpu.make_async_remote_copy(
                src_ref=src.at[side],
                dst_ref=dst.at[side],
                send_sem=ghost_send.at[side, n],
                recv_sem=ghost_recv.at[side, n],
                device_id=target,
                device_id_type=MESH,
            )
            for n, (src, dst) in enumerate(((ghost_out, ghost_in), (ghost_out_ids, ghost_in_ids)))
        ]

    hops = {1: (0, mate), 2: (0, across), 3: (2, mate)}

    def slot_copy(hop, part):
        source, target = hops[hop]
        return pltpu.make_async_remote_copy(
            src_ref=slots.at[source, part],
            dst_ref=slots.at[hop, part],
            send_sem=slot_send.at[hop - 1, part],
            recv_sem=slot_recv.at[hop - 1, part],
            device_id={"col": target},
            device_id_type=MESH,
        )

    def mark_copy(hop):
        source, target = hops[hop]
        return pltpu.make_async_remote_copy(
            src_ref=marks.at[source],
            dst_ref=marks.at[hop],
            send_sem=mark_send.at[hop - 1],
            recv_sem=mark_recv.at[hop - 1],
            device_id={"col": target},
            device_id_type=MESH,
        )

    for side in range(2):
        for copy in ghost_copies(side):
            copy.start()
    for hop in (2, 1):
        mark_copy(hop).start()
        for part in range(PARTS):
            slot_copy(hop, part).start()

    for j in range(height):
        place = wrap(p_cols[j, 0] - start, coarse)
        block = p_ref[j, 0].astype(jnp.float32)
        for g in range(SPAN):
            here = (place >= 4 * g) & (place < 4 * g + 4)
            right[j, :, g * tile : (g + 1) * tile] = (block * jnp.where(here, 1.0, 0.0)).astype(
                jnp.bfloat16
            )
    out_ref[...] = jnp.zeros_like(out_ref)
    for side in range(2):
        for copy in ghost_copies(side):
            copy.wait_recv()
        for t in range(capacity):
            place = wrap(ghost_in_ids[side, t : t + 1] - start, coarse)
            block = ghost_in[side, t].astype(jnp.float32)
            for g in range(SPAN):
                here = jnp.where((place >= 4 * g) & (place < 4 * g + 4), 1.0, 0.0)
                right[height + side * capacity + t, :, g * tile : (g + 1) * tile] = (
                    block * here
                ).astype(jnp.bfloat16)

    def forward(part):
        slot_copy(2, part).wait_recv()
        slot_copy(3, part).start()

    def multiply(i, carry):
        a_copy(i).wait()
        total = None
        for m in range(0, entries, 2):
            ms = range(m, min(m + 2, entries))
            left = jnp.concatenate([a_buf[i, n] for n in ms], axis=1)
            blocks = jnp.concatenate([right[a_cols[i, n]] for n in ms], axis=0)
            term = jnp.dot(left, blocks, preferred_element_type=jnp.float32)
            total = term if total is None else total + term
        grouped[pl.ds(pl.multiple_of(i * tile, tile), tile), :] = total.astype(jnp.bfloat16)
        return carry

    cuts = [0, 6, 11, height]
    for part in range(3):
        lax.fori_loop(cuts[part], cuts[part + 1], multiply, 0)
        if part == 0:
            mark_copy(2).wait_recv()
            mark_copy(3).start()
        forward(part)

    own_column = first_column(s)

    def part_copy(side, o):
        return pltpu.make_async_remote_copy(
            src_ref=part_out.at[side, o],
            dst_ref=part_in.at[side, o],
            send_sem=part_send.at[side, o],
            recv_sem=part_recv.at[side, o],
            device_id={"row": before if side == 0 else after},
            device_id_type=MESH,
        )

    def use_slot(index, slot):
        o = lax.rem(slot + 6 - lax.rem(CB * s, 4), 4)
        total = None
        for part in range(PARTS):
            block = slots[index, part]
            mark = jnp.concatenate(
                [marks[index, part * per_part + n : part * per_part + n + 1] for n in range(per_part)],
                axis=1,
            )
            high = (block.astype(jnp.float32) * mark).astype(jnp.bfloat16)
            left = jnp.concatenate([block - high, high], axis=0)
            depth = per_part * tile
            term = jnp.dot(
                left, grouped[part * depth : (part + 1) * depth], preferred_element_type=jnp.float32
            )
            total = term if total is None else total + term

        @pl.when(o < 2)
        def _():
            part_out[0, o] = total[:tile].astype(jnp.bfloat16)
            part_out[1, o] = total[tile:].astype(jnp.bfloat16)
            for side in range(2):
                part_copy(side, o).start()

        @pl.when(o >= 2)
        def _():
            for g in range(SPAN):
                out_ref[o - 2, lax.rem(own_column + g, column_count)] = total[
                    :tile, g * tile : (g + 1) * tile
                ]

    use_slot(0, k)
    mark_copy(1).wait_recv()
    for part in range(PARTS):
        slot_copy(1, part).wait_recv()
    use_slot(1, mate)
    forward(PARTS - 1)
    use_slot(2, across)
    mark_copy(3).wait_recv()
    for part in range(PARTS):
        slot_copy(3, part).wait_recv()
    use_slot(3, facing)

    for o in range(2):
        for side in range(2):
            part_copy(side, o).wait_recv()
            column = first_column(after if side == 0 else before)
            for g in range(SPAN):
                at = lax.rem(column + g, column_count)
                out_ref[o, at] = out_ref[o, at] + part_in[
                    side, o, :, g * tile : (g + 1) * tile
                ].astype(jnp.float32)

    for side in range(2):
        for copy in ghost_copies(side):
            copy.wait_send()
        for o in range(2):
            part_copy(side, o).wait_send()
    for hop in (1, 2, 3):
        mark_copy(hop).wait_send()
        for part in range(PARTS):
            slot_copy(hop, part).wait_send()


def shards(a_tiles, a_cols, p_tiles, p_cols, send_rows):
    rows, cols = lax.axis_size("row"), lax.axis_size("col")
    assert cols == 4
    height, entries, tile, _ = a_tiles.shape
    capacity = send_rows.shape[1]
    column_count = CB * rows // cols
    width = SPAN * tile
    smem = pl.BlockSpec(memory_space=pltpu.SMEM)
    vmem = pl.BlockSpec(memory_space=pltpu.VMEM)
    bf16, f32, i32 = jnp.bfloat16, jnp.float32, jnp.int32
    dma = pltpu.SemaphoreType.DMA
    return pl.pallas_call(
        functools.partial(kernel, rows),
        out_shape=jax.ShapeDtypeStruct((CB, column_count, tile, tile), f32),
        in_specs=[smem, smem, smem, vmem, pl.BlockSpec(memory_space=pl.ANY)],
        out_specs=vmem,
        scratch_shapes=[
            pltpu.VMEM(a_tiles.shape, bf16),
            pltpu.VMEM((2, capacity, tile, tile), bf16),
            pltpu.VMEM((2, 8, tile), i32),
            pltpu.VMEM((2, capacity, tile, tile), bf16),
            pltpu.VMEM((2, 8, tile), i32),
            pltpu.VMEM((4, PARTS, tile, height // PARTS * tile), bf16),
            pltpu.VMEM((4, height, tile), f32),
            pltpu.VMEM((height + 2 * capacity, tile, width), bf16),
            pltpu.VMEM((height * tile, width), bf16),
            pltpu.VMEM((2, CB, tile, width), bf16),
            pltpu.VMEM((2, CB, tile, width), bf16),
            dma((height,)),
            dma((2, 2)),
            dma((2, 2)),
            dma((3, PARTS)),
            dma((3, PARTS)),
            dma((3,)),
            dma((3,)),
            dma((2, CB)),
            dma((2, CB)),
        ],
        compiler_params=pltpu.CompilerParams(
            collective_id=0, has_side_effects=True, vmem_limit_bytes=48 * 1024 * 1024
        ),
        cost_estimate=pl.CostEstimate(
            flops=2 * height * entries * tile * tile * width,
            bytes_accessed=2 * a_tiles.size,
            transcendentals=0,
        ),
    )(a_cols, p_cols, send_rows, p_tiles, a_tiles)


def solution(mesh):
    in_specs = (
        P("row", None, None, None),
        P("row", None),
        P("row", "col", None, None),
        P("row", "col"),
        P("row", None),
    )
    out_specs = P("row", "col", None, None)
    return jax.shard_map(shards, mesh=mesh, in_specs=in_specs, out_specs=out_specs, check_vma=False)
```

```python
import functools

import jax
import jax.numpy as jnp
from jax import lax
from jax.experimental import pallas as pl
from jax.experimental.pallas import tpu as pltpu
from jax.sharding import PartitionSpec as P

CB = 2
SPAN = 3
PARTS = 4
MESH = pl.DeviceIdType.MESH


def wrap(value, size):
    return jnp.where(value < 0, value + size, value)


def kernel(
    rows,
    a_cols_ref,
    p_cols_ref,
    send_rows_ref,
    p_hbm,
    a_ref,
    out_ref,
    a_cols,
    p_cols,
    send_rows,
    p_ref,
    a_buf,
    ghost_out,
    ghost_out_ids,
    ghost_in,
    ghost_in_ids,
    slots,
    marks,
    right,
    grouped,
    part_out,
    part_in,
    small_sem,
    a_sem,
    ghost_send,
    ghost_recv,
    slot_send,
    slot_recv,
    mark_send,
    mark_recv,
    part_send,
    part_recv,
):
    height, entries, tile = a_buf.shape[0], a_buf.shape[1], a_buf.shape[2]
    capacity = ghost_out.shape[1]
    coarse = CB * rows
    column_count = out_ref.shape[1]
    per_part = height // PARTS
    s = lax.axis_index("row")
    k = lax.axis_index("col")
    after, before = lax.rem(s + 1, rows), lax.rem(s + rows - 1, rows)
    mate = k + 1 - 2 * lax.rem(k, 2)
    across = lax.rem(k + 2, 4)
    facing = 3 - k
    odd = lax.rem(k, 2)
    late = 1 - lax.rem(k // 2 + s, 2)

    def a_copy(i):
        return pltpu.make_async_copy(a_ref.at[i], a_buf.at[i], a_sem.at[i])

    small = [
        pltpu.make_async_copy(source, target, small_sem.at[n])
        for n, (source, target) in enumerate(
            (
                (p_hbm, p_ref),
                (send_rows_ref, send_rows),
                (p_cols_ref, p_cols),
                (a_cols_ref, a_cols),
            )
        )
    ]
    for copy in small:
        copy.start()
    for i in range(height):
        a_copy(i).start()

    barrier = pltpu.get_barrier_semaphore()
    for device in ({"row": before}, {"row": after}, {"col": mate}, {"col": across}):
        pl.semaphore_signal(barrier, inc=1, device_id=device, device_id_type=MESH)

    def first_id(slab):
        return lax.rem(CB * slab + coarse - 4, coarse)

    def first_column(slab):
        start = first_id(slab)
        offset = lax.rem(k + 4 - lax.rem(start, 4), 4)
        return lax.rem((start + offset) // 4, column_count)

    start = first_id(s)
    left_start = lax.rem(CB * s + coarse - 2, coarse)

    for copy in small:
        copy.wait()

    for side in range(2):
        for t in range(capacity):
            row = send_rows[side, t]
            ghost_out[side, t] = p_ref[row, 0]
            ghost_out_ids[side, t : t + 1] = jnp.full((1, tile), p_cols[row], jnp.int32)
    for i in range(height):
        slots[0, i // per_part, :, (i % per_part) * tile : (i % per_part + 1) * tile] = p_ref[i, 0].T
        place = wrap(p_cols[i] - left_start, coarse)
        marks[0, i : i + 1] = jnp.full((1, tile), jnp.where(place >= 4, 1.0, 0.0), jnp.float32)

    pl.semaphore_wait(barrier, 4)

    def ghost_copies(side):
        target = {"row": after if side == 0 else before}
        return [
            pltpu.make_async_remote_copy(
                src_ref=src.at[side],
                dst_ref=dst.at[side],
                send_sem=ghost_send.at[side, n],
                recv_sem=ghost_recv.at[side, n],
                device_id=target,
                device_id_type=MESH,
            )
            for n, (src, dst) in enumerate(((ghost_out, ghost_in), (ghost_out_ids, ghost_in_ids)))
        ]

    hops = {1: (0, mate), 2: (0, across), 3: (2, mate)}

    def slot_copy(hop, part):
        source, target = hops[hop]
        return pltpu.make_async_remote_copy(
            src_ref=slots.at[source, part],
            dst_ref=slots.at[hop, part],
            send_sem=slot_send.at[hop - 1, part],
            recv_sem=slot_recv.at[hop - 1, part],
            device_id={"col": target},
            device_id_type=MESH,
        )

    def mark_copy(hop):
        source, target = hops[hop]
        return pltpu.make_async_remote_copy(
            src_ref=marks.at[source],
            dst_ref=marks.at[hop],
            send_sem=mark_send.at[hop - 1],
            recv_sem=mark_recv.at[hop - 1],
            device_id={"col": target},
            device_id_type=MESH,
        )

    for side in range(2):
        for copy in ghost_copies(side):
            copy.start()
    def send_slot(hop):
        mark_copy(hop).start()
        for part in range(PARTS):
            slot_copy(hop, part).start()

    @pl.when(odd == 0)
    def _():
        send_slot(2)

    send_slot(1)

    for j in range(height):
        place = wrap(p_cols[j] - start, coarse)
        block = p_ref[j, 0].astype(jnp.float32)
        for g in range(SPAN):
            here = (place >= 4 * g) & (place < 4 * g + 4)
            right[j, :, g * tile : (g + 1) * tile] = (block * jnp.where(here, 1.0, 0.0)).astype(
                jnp.bfloat16
            )
    out_ref[...] = jnp.zeros_like(out_ref)
    for side in range(2):
        for copy in ghost_copies(side):
            copy.wait_recv()
        for t in range(capacity):
            place = wrap(ghost_in_ids[side, t : t + 1] - start, coarse)
            block = ghost_in[side, t].astype(jnp.float32)
            for g in range(SPAN):
                here = jnp.where((place >= 4 * g) & (place < 4 * g + 4), 1.0, 0.0)
                right[height + side * capacity + t, :, g * tile : (g + 1) * tile] = (
                    block * here
                ).astype(jnp.bfloat16)

    def forward(part):
        slot_copy(2, part).wait_recv()
        slot_copy(3, part).start()

    def multiply(i, carry):
        a_copy(i).wait()
        total = None
        for m in range(0, entries, 2):
            ms = range(m, min(m + 2, entries))
            left = jnp.concatenate([a_buf[i, n] for n in ms], axis=1)
            blocks = jnp.concatenate([right[a_cols[i, n]] for n in ms], axis=0)
            term = jnp.dot(left, blocks, preferred_element_type=jnp.float32)
            total = term if total is None else total + term
        grouped[pl.ds(pl.multiple_of(i * tile, tile), tile), :] = total.astype(jnp.bfloat16)
        return carry

    lax.fori_loop(0, height // 2, multiply, 0)

    @pl.when(odd == 1)
    def _():
        send_slot(2)

    @pl.when(odd == 0)
    def _():
        mark_copy(2).wait_recv()
        mark_copy(3).start()
        forward(0)
        forward(1)

    lax.fori_loop(height // 2, height * 3 // 4, multiply, 0)

    @pl.when(odd == 0)
    def _():
        forward(2)
        forward(3)

    lax.fori_loop(height * 3 // 4, height, multiply, 0)

    own_column = first_column(s)

    def part_copy(side, o, count):
        return pltpu.make_async_remote_copy(
            src_ref=part_out.at[side, o, pl.ds(0, count)],
            dst_ref=part_in.at[side, o, pl.ds(0, count)],
            send_sem=part_send.at[side, o],
            recv_sem=part_recv.at[side, o],
            device_id={"row": before if side == 0 else after},
            device_id_type=MESH,
        )

    def facing_ready():
        mark_copy(3).wait_recv()
        for part in range(PARTS):
            slot_copy(3, part).wait_recv()

    def even_ready():
        @pl.when(odd == 1)
        def _():
            facing_ready()

    def odd_ready():
        @pl.when(odd == 1)
        def _():
            mark_copy(2).wait_recv()
            mark_copy(3).start()
            for part in range(PARTS):
                forward(part)

        @pl.when(odd == 0)
        def _():
            facing_ready()

    def use_slot(index, o):
        total = None
        for part in range(PARTS):
            left = slots[index, part]
            if o < 2:
                mark = jnp.concatenate(
                    [marks[index, part * per_part + n : part * per_part + n + 1] for n in range(per_part)],
                    axis=1,
                )
                high = (left.astype(jnp.float32) * mark).astype(jnp.bfloat16)
                left = jnp.concatenate([left - high, high], axis=0)
            depth = per_part * tile
            term = jnp.dot(
                left, grouped[part * depth : (part + 1) * depth], preferred_element_type=jnp.float32
            )
            total = term if total is None else total + term
        for g in range(SPAN):
            columns = slice(g * tile, (g + 1) * tile)
            if o < 2:
                part_out[0, o, g] = total[:tile, columns].astype(jnp.bfloat16)
                part_out[1, o, g] = total[tile:, columns].astype(jnp.bfloat16)
            else:
                out_ref[o - 2, lax.rem(own_column + g, column_count)] = total[:, columns]
        if o < 2:
            for count in (SPAN, SPAN - 1):

                @pl.when(late == (1 if count == SPAN else 0))
                def _():
                    for side in range(2):
                        part_copy(side, o, count).start()

    def when_late(value, action):
        @pl.when(late == value)
        def _():
            action()

    mark_copy(1).wait_recv()
    for part in range(PARTS):
        slot_copy(1, part).wait_recv()
    when_late(1, even_ready)
    use_slot(2 * late + odd, 0)
    when_late(1, odd_ready)
    use_slot(2 * late + 1 - odd, 1)
    when_late(0, even_ready)
    use_slot(2 - 2 * late + odd, 2)
    when_late(0, odd_ready)
    use_slot(3 - 2 * late - odd, 3)

    def collect(count):
        for o in range(2):
            for side in range(2):
                part_copy(side, o, count).wait_recv()
                column = first_column(after if side == 0 else before)
                for g in range(count):
                    at = lax.rem(column + g, column_count)
                    out_ref[o, at] = out_ref[o, at] + part_in[side, o, g].astype(jnp.float32)

    when_late(0, lambda: collect(SPAN))
    when_late(1, lambda: collect(SPAN - 1))

    def sent(count):
        for side in range(2):
            for o in range(2):
                part_copy(side, o, count).wait_send()

    when_late(1, lambda: sent(SPAN))
    when_late(0, lambda: sent(SPAN - 1))
    for side in range(2):
        for copy in ghost_copies(side):
            copy.wait_send()
    for hop in (1, 2, 3):
        mark_copy(hop).wait_send()
        for part in range(PARTS):
            slot_copy(hop, part).wait_send()


def shards(a_tiles, a_cols, p_tiles, p_cols, send_rows):
    rows, cols = lax.axis_size("row"), lax.axis_size("col")
    assert cols == 4
    height, entries, tile, _ = a_tiles.shape
    capacity = send_rows.shape[1]
    column_count = CB * rows // cols
    width = SPAN * tile
    vmem = pl.BlockSpec(memory_space=pltpu.VMEM)
    bf16, f32, i32 = jnp.bfloat16, jnp.float32, jnp.int32
    dma = pltpu.SemaphoreType.DMA
    return pl.pallas_call(
        functools.partial(kernel, rows),
        out_shape=jax.ShapeDtypeStruct((CB, column_count, tile, tile), f32),
        in_specs=[pl.BlockSpec(memory_space=pltpu.HBM)] * 5,
        out_specs=vmem,
        scratch_shapes=[
            pltpu.SMEM(a_cols.shape, i32),
            pltpu.SMEM((height,), i32),
            pltpu.SMEM(send_rows.shape, i32),
            pltpu.VMEM(p_tiles.shape, bf16),
            pltpu.VMEM(a_tiles.shape, bf16),
            pltpu.VMEM((2, capacity, tile, tile), bf16),
            pltpu.VMEM((2, 8, tile), i32),
            pltpu.VMEM((2, capacity, tile, tile), bf16),
            pltpu.VMEM((2, 8, tile), i32),
            pltpu.VMEM((4, PARTS, tile, height // PARTS * tile), bf16),
            pltpu.VMEM((4, height, tile), f32),
            pltpu.VMEM((height + 2 * capacity, tile, width), bf16),
            pltpu.VMEM((height * tile, width), bf16),
            pltpu.VMEM((2, CB, SPAN, tile, tile), bf16),
            pltpu.VMEM((2, CB, SPAN, tile, tile), bf16),
            dma((4,)),
            dma((height,)),
            dma((2, 2)),
            dma((2, 2)),
            dma((3, PARTS)),
            dma((3, PARTS)),
            dma((3,)),
            dma((3,)),
            dma((2, CB)),
            dma((2, CB)),
        ],
        compiler_params=pltpu.CompilerParams(
            collective_id=0, has_side_effects=True, vmem_limit_bytes=64 * 1024 * 1024
        ),
        cost_estimate=pl.CostEstimate(
            flops=2 * height * entries * tile * tile * width,
            bytes_accessed=2 * a_tiles.size,
            transcendentals=0,
        ),
    )(a_cols, p_cols.reshape(height), send_rows, p_tiles, a_tiles)


def solution(mesh):
    in_specs = (
        P("row", None, None, None),
        P("row", None),
        P("row", "col", None, None),
        P("row", "col"),
        P("row", None),
    )
    out_specs = P("row", "col", None, None)
    return jax.shard_map(shards, mesh=mesh, in_specs=in_specs, out_specs=out_specs, check_vma=False)
```

```python
import functools

import jax
import jax.numpy as jnp
from jax import lax
from jax.experimental import pallas as pl
from jax.experimental.pallas import tpu as pltpu
from jax.sharding import PartitionSpec as P

CB = 2
SPAN = 3
PARTS = 4
MESH = pl.DeviceIdType.MESH


def wrap(value, size):
    return jnp.where(value < 0, value + size, value)


def kernel(
    rows,
    a_cols_ref,
    p_cols_ref,
    send_rows_ref,
    p_hbm,
    a_ref,
    out_ref,
    a_cols,
    p_cols,
    send_rows,
    p_ref,
    a_buf,
    ghost_out,
    ghost_out_ids,
    ghost_in,
    ghost_in_ids,
    slots,
    marks,
    blocks,
    running,
    table_v,
    table,
    grouped,
    part_out,
    part_in,
    small_sem,
    table_sem,
    a_sem,
    ghost_send,
    ghost_recv,
    slot_send,
    slot_recv,
    mark_send,
    mark_recv,
    part_send,
    part_recv,
):
    height, entries, tile = a_buf.shape[0], a_buf.shape[1], a_buf.shape[2]
    capacity = ghost_out.shape[1]
    coarse = CB * rows
    column_count = out_ref.shape[1]
    per_part = height // PARTS
    s = lax.axis_index("row")
    k = lax.axis_index("col")
    after, before = lax.rem(s + 1, rows), lax.rem(s + rows - 1, rows)
    mate = k + 1 - 2 * lax.rem(k, 2)
    across = lax.rem(k + 2, 4)
    facing = 3 - k
    odd = lax.rem(k, 2)
    late = 1 - lax.rem(k // 2 + s, 2)

    def a_copy(i):
        return pltpu.make_async_copy(a_ref.at[i], a_buf.at[i], a_sem.at[i])

    small = [
        pltpu.make_async_copy(source, target, small_sem.at[n])
        for n, (source, target) in enumerate(
            (
                (p_hbm, p_ref),
                (send_rows_ref, send_rows),
                (p_cols_ref, p_cols),
                (a_cols_ref, a_cols),
            )
        )
    ]
    for copy in small:
        copy.start()
    for i in range(height):
        a_copy(i).start()

    barrier = pltpu.get_barrier_semaphore()
    for device in ({"row": before}, {"row": after}, {"col": mate}, {"col": across}):
        pl.semaphore_signal(barrier, inc=1, device_id=device, device_id_type=MESH)

    def first_id(slab):
        return lax.rem(CB * slab + coarse - 4, coarse)

    def first_column(slab):
        start = first_id(slab)
        offset = lax.rem(k + 4 - lax.rem(start, 4), 4)
        return lax.rem((start + offset) // 4, column_count)

    start = first_id(s)
    left_start = lax.rem(CB * s + coarse - 2, coarse)

    for copy in small:
        copy.wait()

    for side in range(2):
        for t in range(capacity):
            row = send_rows[side, t]
            ghost_out[side, t] = p_ref[row, 0]
            ghost_out_ids[side, t : t + 1] = jnp.full((1, tile), p_cols[row], jnp.int32)
    for i in range(height):
        slots[0, i // per_part, :, (i % per_part) * tile : (i % per_part + 1) * tile] = p_ref[i, 0].T
        place = wrap(p_cols[i] - left_start, coarse)
        marks[0, i : i + 1] = jnp.full((1, tile), jnp.where(place >= 4, 1.0, 0.0), jnp.float32)

    pl.semaphore_wait(barrier, 4)

    def ghost_copies(side):
        target = {"row": after if side == 0 else before}
        return [
            pltpu.make_async_remote_copy(
                src_ref=src.at[side],
                dst_ref=dst.at[side],
                send_sem=ghost_send.at[side, n],
                recv_sem=ghost_recv.at[side, n],
                device_id=target,
                device_id_type=MESH,
            )
            for n, (src, dst) in enumerate(((ghost_out, ghost_in), (ghost_out_ids, ghost_in_ids)))
        ]

    hops = {1: (0, mate), 2: (0, across), 3: (2, mate)}

    def slot_copy(hop, part):
        source, target = hops[hop]
        return pltpu.make_async_remote_copy(
            src_ref=slots.at[source, part],
            dst_ref=slots.at[hop, part],
            send_sem=slot_send.at[hop - 1, part],
            recv_sem=slot_recv.at[hop - 1, part],
            device_id={"col": target},
            device_id_type=MESH,
        )

    def mark_copy(hop):
        source, target = hops[hop]
        return pltpu.make_async_remote_copy(
            src_ref=marks.at[source],
            dst_ref=marks.at[hop],
            send_sem=mark_send.at[hop - 1],
            recv_sem=mark_recv.at[hop - 1],
            device_id={"col": target},
            device_id_type=MESH,
        )

    for side in range(2):
        for copy in ghost_copies(side):
            copy.start()
    def send_slot(hop):
        mark_copy(hop).start()
        for part in range(PARTS):
            slot_copy(hop, part).start()

    @pl.when(odd == 0)
    def _():
        send_slot(2)

    send_slot(1)

    zero_block = height + 2 * capacity
    pairs = (entries + SPAN) // 2
    listed = a_cols[...]
    group = jnp.zeros_like(listed)

    def place_group(place):
        return jnp.where(place >= 4, 1, 0) + jnp.where(place >= 8, 1, 0)

    for j in range(height):
        blocks[j] = p_ref[j, 0]
        group = group + jnp.where(listed == j, place_group(wrap(p_cols[j] - start, coarse)), 0)
    blocks[zero_block] = jnp.zeros_like(blocks[zero_block])
    running[pairs] = jnp.zeros_like(running[pairs])
    out_ref[...] = jnp.zeros_like(out_ref)
    for side in range(2):
        for copy in ghost_copies(side):
            copy.wait_recv()
        for t in range(capacity):
            j = height + side * capacity + t
            blocks[j] = ghost_in[side, t]
            place = wrap(ghost_in_ids[side, t : t + 1, :entries] - start, coarse)
            group = group + jnp.where(listed == j, place_group(place), 0)

    lane = lax.broadcasted_iota(jnp.int32, listed.shape, 1)
    rank = jnp.zeros_like(listed)
    counts = [jnp.zeros((height, 1), jnp.int32) for _ in range(SPAN)]
    for m in range(entries):
        one = group[:, m : m + 1]
        rank = rank + jnp.where((group == one) & (lane > m), 1, 0)
        counts = [counts[g] + jnp.where(one == g, 1, 0) for g in range(SPAN)]
    sizes = [((c + 1) >> 1) << 1 for c in counts]
    starts = [jnp.zeros_like(sizes[0]), sizes[0], sizes[0] + sizes[1]]
    slot = rank
    for g in range(SPAN):
        slot = slot + jnp.where(group == g, starts[g], 0)
    wide = table_v.shape[1:]
    place = lax.broadcasted_iota(jnp.int32, wide, 1)
    chosen = jnp.zeros(wide, jnp.int32)
    column = jnp.full(wide, zero_block, jnp.int32)
    for m in range(entries):
        here = slot[:, m : m + 1] == place
        chosen = chosen + jnp.where(here, m, 0)
        column = column + jnp.where(here, listed[:, m : m + 1] - zero_block, 0)
    going = jnp.ones(wide, jnp.int32)
    for g in range(SPAN):
        going = jnp.where(2 * place == starts[g], 0, going)
        last = jnp.where(counts[g] > 0, ((starts[g] + sizes[g]) >> 1) - 1, pairs)
        going = jnp.where(place == 64 + g, last, going)
    table_v[0] = chosen
    table_v[1] = column
    table_v[2] = going
    table_copy = pltpu.make_async_copy(table_v, table, table_sem)
    table_copy.start()
    table_copy.wait()

    def forward(part):
        slot_copy(2, part).wait_recv()
        slot_copy(3, part).start()

    for i in range(height):
        a_copy(i).wait()

    def multiply(i, carry):
        total = None
        for pair in range(pairs):
            at = (2 * pair, 2 * pair + 1)
            left = jnp.concatenate([a_buf[i, table[0, i, n]] for n in at], axis=1)
            right = jnp.concatenate([blocks[table[1, i, n]] for n in at], axis=0)
            term = jnp.dot(left, right, preferred_element_type=jnp.float32)
            total = term if pair == 0 else jnp.where(table[2, i, pair] > 0, total, 0.0) + term
            running[pair] = total
        rows_of = pl.ds(pl.multiple_of(i * tile, tile), tile)
        for g in range(SPAN):
            grouped[rows_of, g * tile : (g + 1) * tile] = running[table[2, i, 64 + g]].astype(jnp.bfloat16)
        return carry

    lax.fori_loop(0, height // 2, multiply, 0)

    @pl.when(odd == 1)
    def _():
        send_slot(2)

    @pl.when(odd == 0)
    def _():
        mark_copy(2).wait_recv()
        mark_copy(3).start()
        forward(0)
        forward(1)

    lax.fori_loop(height // 2, height * 3 // 4, multiply, 0)

    @pl.when(odd == 0)
    def _():
        forward(2)
        forward(3)

    lax.fori_loop(height * 3 // 4, height, multiply, 0)

    own_column = first_column(s)

    def part_copy(side, o, count):
        return pltpu.make_async_remote_copy(
            src_ref=part_out.at[side, o, pl.ds(0, count)],
            dst_ref=part_in.at[side, o, pl.ds(0, count)],
            send_sem=part_send.at[side, o],
            recv_sem=part_recv.at[side, o],
            device_id={"row": before if side == 0 else after},
            device_id_type=MESH,
        )

    def facing_ready():
        mark_copy(3).wait_recv()
        for part in range(PARTS):
            slot_copy(3, part).wait_recv()

    def even_ready():
        @pl.when(odd == 1)
        def _():
            facing_ready()

    def odd_ready():
        @pl.when(odd == 1)
        def _():
            mark_copy(2).wait_recv()
            mark_copy(3).start()
            for part in range(PARTS):
                forward(part)

        @pl.when(odd == 0)
        def _():
            facing_ready()

    def use_slot(index, o):
        total = None
        for part in range(PARTS):
            left = slots[index, part]
            if o < 2:
                mark = jnp.concatenate(
                    [marks[index, part * per_part + n : part * per_part + n + 1] for n in range(per_part)],
                    axis=1,
                )
                high = (left.astype(jnp.float32) * mark).astype(jnp.bfloat16)
                left = jnp.concatenate([left - high, high], axis=0)
            depth = per_part * tile
            term = jnp.dot(
                left, grouped[part * depth : (part + 1) * depth], preferred_element_type=jnp.float32
            )
            total = term if total is None else total + term
        for g in range(SPAN):
            columns = slice(g * tile, (g + 1) * tile)
            if o < 2:
                part_out[0, o, g] = total[:tile, columns].astype(jnp.bfloat16)
                part_out[1, o, g] = total[tile:, columns].astype(jnp.bfloat16)
            else:
                out_ref[o - 2, lax.rem(own_column + g, column_count)] = total[:, columns]
        if o < 2:
            for count in (SPAN, SPAN - 1):

                @pl.when(late == (1 if count == SPAN else 0))
                def _():
                    for side in range(2):
                        part_copy(side, o, count).start()

    def when_late(value, action):
        @pl.when(late == value)
        def _():
            action()

    mark_copy(1).wait_recv()
    for part in range(PARTS):
        slot_copy(1, part).wait_recv()
    when_late(1, even_ready)
    use_slot(2 * late + odd, 0)
    when_late(1, odd_ready)
    use_slot(2 * late + 1 - odd, 1)
    when_late(0, even_ready)
    use_slot(2 - 2 * late + odd, 2)
    when_late(0, odd_ready)
    use_slot(3 - 2 * late - odd, 3)

    def collect(count):
        for o in range(2):
            for side in range(2):
                part_copy(side, o, count).wait_recv()
                column = first_column(after if side == 0 else before)
                for g in range(count):
                    at = lax.rem(column + g, column_count)
                    out_ref[o, at] = out_ref[o, at] + part_in[side, o, g].astype(jnp.float32)

    when_late(0, lambda: collect(SPAN))
    when_late(1, lambda: collect(SPAN - 1))

    def sent(count):
        for side in range(2):
            for o in range(2):
                part_copy(side, o, count).wait_send()

    when_late(1, lambda: sent(SPAN))
    when_late(0, lambda: sent(SPAN - 1))
    for side in range(2):
        for copy in ghost_copies(side):
            copy.wait_send()
    for hop in (1, 2, 3):
        mark_copy(hop).wait_send()
        for part in range(PARTS):
            slot_copy(hop, part).wait_send()


def shards(a_tiles, a_cols, p_tiles, p_cols, send_rows):
    rows, cols = lax.axis_size("row"), lax.axis_size("col")
    assert cols == 4
    height, entries, tile, _ = a_tiles.shape
    capacity = send_rows.shape[1]
    column_count = CB * rows // cols
    width = SPAN * tile
    vmem = pl.BlockSpec(memory_space=pltpu.VMEM)
    operands = (a_cols, p_cols.reshape(height), send_rows, p_tiles, a_tiles)
    bf16, f32, i32 = jnp.bfloat16, jnp.float32, jnp.int32
    dma = pltpu.SemaphoreType.DMA
    return pl.pallas_call(
        functools.partial(kernel, rows),
        out_shape=jax.ShapeDtypeStruct((CB, column_count, tile, tile), f32),
        in_specs=[pl.BlockSpec(memory_space=pltpu.HBM)] * 5,
        out_specs=vmem,
        scratch_shapes=[
            pltpu.VMEM(a_cols.shape, i32),
            pltpu.SMEM((height,), i32),
            pltpu.SMEM(send_rows.shape, i32),
            pltpu.VMEM(p_tiles.shape, bf16),
            pltpu.VMEM(a_tiles.shape, bf16),
            pltpu.VMEM((2, capacity, tile, tile), bf16),
            pltpu.VMEM((2, 8, tile), i32),
            pltpu.VMEM((2, capacity, tile, tile), bf16),
            pltpu.VMEM((2, 8, tile), i32),
            pltpu.VMEM((4, PARTS, tile, height // PARTS * tile), bf16),
            pltpu.VMEM((4, height, tile), f32),
            pltpu.VMEM((height + 2 * capacity + 1, tile, tile), bf16),
            pltpu.VMEM(((entries + SPAN) // 2 + 1, tile, tile), f32),
            pltpu.VMEM((3, height, 128), i32),
            pltpu.SMEM((3, height, 128), i32),
            pltpu.VMEM((height * tile, width), bf16),
            pltpu.VMEM((2, CB, SPAN, tile, tile), bf16),
            pltpu.VMEM((2, CB, SPAN, tile, tile), bf16),
            dma((4,)),
            dma,
            dma((height,)),
            dma((2, 2)),
            dma((2, 2)),
            dma((3, PARTS)),
            dma((3, PARTS)),
            dma((3,)),
            dma((3,)),
            dma((2, CB)),
            dma((2, CB)),
        ],
        compiler_params=pltpu.CompilerParams(
            collective_id=0, has_side_effects=True, vmem_limit_bytes=48 * 1024 * 1024
        ),
        cost_estimate=pl.CostEstimate(
            flops=2 * height * entries * tile * tile * width,
            bytes_accessed=2 * a_tiles.size,
            transcendentals=0,
        ),
    )(*(pltpu.with_memory_space_constraint(x, pltpu.HBM) for x in operands))


def solution(mesh):
    in_specs = (
        P("row", None, None, None),
        P("row", None),
        P("row", "col", None, None),
        P("row", "col"),
        P("row", None),
    )
    out_specs = P("row", "col", None, None)
    return jax.shard_map(shards, mesh=mesh, in_specs=in_specs, out_specs=out_specs, check_vma=False)
```

```python
import functools

import jax
import jax.numpy as jnp
from jax import lax
from jax.experimental import pallas as pl
from jax.experimental.pallas import tpu as pltpu
from jax.sharding import PartitionSpec as P

CB = 2
SPAN = 3
PARTS = 4
MESH = pl.DeviceIdType.MESH


def wrap(value, size):
    return jnp.where(value < 0, value + size, value)


def kernel(
    rows,
    a_cols_ref,
    p_cols_ref,
    send_rows_ref,
    p_hbm,
    a_ref,
    out_ref,
    a_cols,
    p_cols,
    send_rows,
    p_ref,
    a_buf,
    ghost_out,
    ghost_out_ids,
    ghost_in,
    ghost_in_ids,
    slots,
    marks,
    blocks,
    running,
    table_v,
    table,
    grouped,
    part_out,
    part_in,
    small_sem,
    table_sem,
    a_sem,
    ghost_send,
    ghost_recv,
    slot_send,
    slot_recv,
    mark_send,
    mark_recv,
    part_send,
    part_recv,
):
    height, entries, tile = a_buf.shape[0], a_buf.shape[1], a_buf.shape[2]
    capacity = ghost_out.shape[1]
    coarse = CB * rows
    column_count = out_ref.shape[1]
    per_part = height // PARTS
    s = lax.axis_index("row")
    k = lax.axis_index("col")
    after, before = lax.rem(s + 1, rows), lax.rem(s + rows - 1, rows)
    mate = k + 1 - 2 * lax.rem(k, 2)
    across = lax.rem(k + 2, 4)
    facing = 3 - k
    odd = lax.rem(k, 2)
    late = 1 - lax.rem(k // 2 + s, 2)

    barrier = pltpu.get_barrier_semaphore()
    for device in ({"row": before}, {"row": after}, {"col": mate}, {"col": across}):
        pl.semaphore_signal(barrier, inc=1, device_id=device, device_id_type=MESH)

    def a_copy(i):
        return pltpu.make_async_copy(a_ref.at[i], a_buf.at[i], a_sem.at[i])

    small = [
        pltpu.make_async_copy(source, target, small_sem.at[n])
        for n, (source, target) in enumerate(
            (
                (p_hbm, p_ref),
                (send_rows_ref, send_rows),
                (p_cols_ref, p_cols),
                (a_cols_ref, a_cols),
            )
        )
    ]
    for copy in small:
        copy.start()
    for i in range(height):
        a_copy(i).start()

    def first_id(slab):
        return lax.rem(CB * slab + coarse - 4, coarse)

    def first_column(slab):
        start = first_id(slab)
        offset = lax.rem(k + 4 - lax.rem(start, 4), 4)
        return lax.rem((start + offset) // 4, column_count)

    start = first_id(s)
    left_start = lax.rem(CB * s + coarse - 2, coarse)

    for copy in small:
        copy.wait()

    for side in range(2):
        for t in range(capacity):
            row = send_rows[side, t]
            ghost_out[side, t] = p_ref[row, 0]
            ghost_out_ids[side, t : t + 1] = jnp.full((1, tile), p_cols[row], jnp.int32)
    for i in range(height):
        slots[0, i // per_part, :, (i % per_part) * tile : (i % per_part + 1) * tile] = p_ref[i, 0].T
        place = wrap(p_cols[i] - left_start, coarse)
        marks[0, i : i + 1] = jnp.full((1, tile), jnp.where(place >= 4, 1.0, 0.0), jnp.float32)

    pl.semaphore_wait(barrier, 4)

    def ghost_copies(side):
        target = {"row": after if side == 0 else before}
        return [
            pltpu.make_async_remote_copy(
                src_ref=src.at[side],
                dst_ref=dst.at[side],
                send_sem=ghost_send.at[side, n],
                recv_sem=ghost_recv.at[side, n],
                device_id=target,
                device_id_type=MESH,
            )
            for n, (src, dst) in enumerate(((ghost_out, ghost_in), (ghost_out_ids, ghost_in_ids)))
        ]

    hops = {1: (0, mate), 2: (0, across), 3: (2, mate)}

    def slot_copy(hop, part):
        source, target = hops[hop]
        return pltpu.make_async_remote_copy(
            src_ref=slots.at[source, part],
            dst_ref=slots.at[hop, part],
            send_sem=slot_send.at[hop - 1, part],
            recv_sem=slot_recv.at[hop - 1, part],
            device_id={"col": target},
            device_id_type=MESH,
        )

    def mark_copy(hop):
        source, target = hops[hop]
        return pltpu.make_async_remote_copy(
            src_ref=marks.at[source],
            dst_ref=marks.at[hop],
            send_sem=mark_send.at[hop - 1],
            recv_sem=mark_recv.at[hop - 1],
            device_id={"col": target},
            device_id_type=MESH,
        )

    for side in range(2):
        for copy in ghost_copies(side):
            copy.start()
    def send_slot(hop):
        mark_copy(hop).start()
        for part in range(PARTS):
            slot_copy(hop, part).start()

    @pl.when(odd == 0)
    def _():
        send_slot(2)

    send_slot(1)

    zero_block = height + 2 * capacity
    pairs = (entries + SPAN) // 2
    listed = a_cols[...]
    group = jnp.zeros_like(listed)

    def place_group(place):
        return jnp.where(place >= 4, 1, 0) + jnp.where(place >= 8, 1, 0)

    for j in range(height):
        blocks[j] = p_ref[j, 0]
        group = group + jnp.where(listed == j, place_group(wrap(p_cols[j] - start, coarse)), 0)
    blocks[zero_block] = jnp.zeros_like(blocks[zero_block])
    running[pairs] = jnp.zeros_like(running[pairs])
    out_ref[...] = jnp.zeros_like(out_ref)
    for side in range(2):
        for copy in ghost_copies(side):
            copy.wait_recv()
        for t in range(capacity):
            j = height + side * capacity + t
            blocks[j] = ghost_in[side, t]
            place = wrap(ghost_in_ids[side, t : t + 1, :entries] - start, coarse)
            group = group + jnp.where(listed == j, place_group(place), 0)

    lane = lax.broadcasted_iota(jnp.int32, listed.shape, 1)
    rank = jnp.zeros_like(listed)
    counts = [jnp.zeros((height, 1), jnp.int32) for _ in range(SPAN)]
    for m in range(entries):
        one = group[:, m : m + 1]
        rank = rank + jnp.where((group == one) & (lane > m), 1, 0)
        counts = [counts[g] + jnp.where(one == g, 1, 0) for g in range(SPAN)]
    sizes = [((c + 1) >> 1) << 1 for c in counts]
    starts = [jnp.zeros_like(sizes[0]), sizes[0], sizes[0] + sizes[1]]
    slot = rank
    for g in range(SPAN):
        slot = slot + jnp.where(group == g, starts[g], 0)
    wide = table_v.shape[1:]
    place = lax.broadcasted_iota(jnp.int32, wide, 1)
    chosen = jnp.zeros(wide, jnp.int32)
    column = jnp.full(wide, zero_block, jnp.int32)
    for m in range(entries):
        here = slot[:, m : m + 1] == place
        chosen = chosen + jnp.where(here, m, 0)
        column = column + jnp.where(here, listed[:, m : m + 1] - zero_block, 0)
    going = jnp.ones(wide, jnp.int32)
    for g in range(SPAN):
        going = jnp.where(2 * place == starts[g], 0, going)
        last = jnp.where(counts[g] > 0, ((starts[g] + sizes[g]) >> 1) - 1, pairs)
        going = jnp.where(place == 64 + g, last, going)
    table_v[0] = chosen
    table_v[1] = column
    table_v[2] = going
    table_copy = pltpu.make_async_copy(table_v, table, table_sem)
    table_copy.start()

    @pl.when(odd == 1)
    def _():
        send_slot(2)

    table_copy.wait()

    def forward(part):
        slot_copy(2, part).wait_recv()
        slot_copy(3, part).start()

    for i in range(height):
        a_copy(i).wait()

    def multiply(i, carry):
        total = None
        for pair in range(pairs):
            at = (2 * pair, 2 * pair + 1)
            left = jnp.concatenate([a_buf[i, table[0, i, n]] for n in at], axis=1)
            right = jnp.concatenate([blocks[table[1, i, n]] for n in at], axis=0)
            term = jnp.dot(left, right, preferred_element_type=jnp.float32)
            total = term if pair == 0 else jnp.where(table[2, i, pair] > 0, total, 0.0) + term
            running[pair] = total
        rows_of = pl.ds(pl.multiple_of(i * tile, tile), tile)
        for g in range(SPAN):
            grouped[rows_of, g * tile : (g + 1) * tile] = running[table[2, i, 64 + g]].astype(jnp.bfloat16)
        return carry

    lax.fori_loop(0, height // 2, multiply, 0)

    @pl.when(odd == 0)
    def _():
        mark_copy(2).wait_recv()
        mark_copy(3).start()
        forward(0)
        forward(1)

    lax.fori_loop(height // 2, height * 3 // 4, multiply, 0)

    @pl.when(odd == 0)
    def _():
        forward(2)
        forward(3)

    lax.fori_loop(height * 3 // 4, height, multiply, 0)

    @pl.when(odd == 1)
    def _():
        mark_copy(2).wait_recv()
        mark_copy(3).start()
        for part in range(PARTS - 1):
            forward(part)

    own_column = first_column(s)

    def part_copy(side, o, count):
        return pltpu.make_async_remote_copy(
            src_ref=part_out.at[side, o, pl.ds(0, count)],
            dst_ref=part_in.at[side, o, pl.ds(0, count)],
            send_sem=part_send.at[side, o],
            recv_sem=part_recv.at[side, o],
            device_id={"row": before if side == 0 else after},
            device_id_type=MESH,
        )

    def facing_ready():
        mark_copy(3).wait_recv()
        for part in range(PARTS):
            slot_copy(3, part).wait_recv()

    def even_ready():
        @pl.when(odd == 1)
        def _():
            facing_ready()

    def odd_ready():
        @pl.when(odd == 1)
        def _():
            forward(PARTS - 1)

        @pl.when(odd == 0)
        def _():
            facing_ready()

    def use_slot(index, o):
        total = None
        for part in range(PARTS):
            left = slots[index, part]
            if o < 2:
                mark = jnp.concatenate(
                    [marks[index, part * per_part + n : part * per_part + n + 1] for n in range(per_part)],
                    axis=1,
                )
                high = (left.astype(jnp.float32) * mark).astype(jnp.bfloat16)
                left = jnp.concatenate([left - high, high], axis=0)
            depth = per_part * tile
            term = jnp.dot(
                left, grouped[part * depth : (part + 1) * depth], preferred_element_type=jnp.float32
            )
            total = term if total is None else total + term
        for g in range(SPAN):
            columns = slice(g * tile, (g + 1) * tile)
            if o < 2:
                part_out[0, o, g] = total[:tile, columns].astype(jnp.bfloat16)
                part_out[1, o, g] = total[tile:, columns].astype(jnp.bfloat16)
            else:
                out_ref[o - 2, lax.rem(own_column + g, column_count)] = total[:, columns]
        if o < 2:
            for count in (SPAN, SPAN - 1):

                @pl.when(late == (1 if count == SPAN else 0))
                def _():
                    for side in range(2):
                        part_copy(side, o, count).start()

    def when_late(value, action):
        @pl.when(late == value)
        def _():
            action()

    mark_copy(1).wait_recv()
    for part in range(PARTS):
        slot_copy(1, part).wait_recv()
    when_late(1, even_ready)
    use_slot(2 * late + odd, 0)
    when_late(1, odd_ready)
    use_slot(2 * late + 1 - odd, 1)
    when_late(0, even_ready)
    use_slot(2 - 2 * late + odd, 2)
    when_late(0, odd_ready)
    use_slot(3 - 2 * late - odd, 3)

    def collect(count):
        for o in range(2):
            for side in range(2):
                part_copy(side, o, count).wait_recv()
                column = first_column(after if side == 0 else before)
                for g in range(count):
                    at = lax.rem(column + g, column_count)
                    out_ref[o, at] = out_ref[o, at] + part_in[side, o, g].astype(jnp.float32)

    when_late(0, lambda: collect(SPAN))
    when_late(1, lambda: collect(SPAN - 1))

    def sent(count):
        for side in range(2):
            for o in range(2):
                part_copy(side, o, count).wait_send()

    when_late(1, lambda: sent(SPAN))
    when_late(0, lambda: sent(SPAN - 1))
    for side in range(2):
        for copy in ghost_copies(side):
            copy.wait_send()
    for hop in (1, 2, 3):
        mark_copy(hop).wait_send()
        for part in range(PARTS):
            slot_copy(hop, part).wait_send()


def shards(a_tiles, a_cols, p_tiles, p_cols, send_rows):
    rows, cols = lax.axis_size("row"), lax.axis_size("col")
    assert cols == 4
    height, entries, tile, _ = a_tiles.shape
    capacity = send_rows.shape[1]
    column_count = CB * rows // cols
    width = SPAN * tile
    vmem = pl.BlockSpec(memory_space=pltpu.VMEM)
    operands = (a_cols, p_cols.reshape(height), send_rows, p_tiles, a_tiles)
    bf16, f32, i32 = jnp.bfloat16, jnp.float32, jnp.int32
    dma = pltpu.SemaphoreType.DMA
    return pl.pallas_call(
        functools.partial(kernel, rows),
        out_shape=jax.ShapeDtypeStruct((CB, column_count, tile, tile), f32),
        in_specs=[pl.BlockSpec(memory_space=pltpu.HBM)] * 5,
        out_specs=vmem,
        scratch_shapes=[
            pltpu.VMEM(a_cols.shape, i32),
            pltpu.SMEM((height,), i32),
            pltpu.SMEM(send_rows.shape, i32),
            pltpu.VMEM(p_tiles.shape, bf16),
            pltpu.VMEM(a_tiles.shape, bf16),
            pltpu.VMEM((2, capacity, tile, tile), bf16),
            pltpu.VMEM((2, 8, tile), i32),
            pltpu.VMEM((2, capacity, tile, tile), bf16),
            pltpu.VMEM((2, 8, tile), i32),
            pltpu.VMEM((4, PARTS, tile, height // PARTS * tile), bf16),
            pltpu.VMEM((4, height, tile), f32),
            pltpu.VMEM((height + 2 * capacity + 1, tile, tile), bf16),
            pltpu.VMEM(((entries + SPAN) // 2 + 1, tile, tile), f32),
            pltpu.VMEM((3, height, 128), i32),
            pltpu.SMEM((3, height, 128), i32),
            pltpu.VMEM((height * tile, width), bf16),
            pltpu.VMEM((2, CB, SPAN, tile, tile), bf16),
            pltpu.VMEM((2, CB, SPAN, tile, tile), bf16),
            dma((4,)),
            dma,
            dma((height,)),
            dma((2, 2)),
            dma((2, 2)),
            dma((3, PARTS)),
            dma((3, PARTS)),
            dma((3,)),
            dma((3,)),
            dma((2, CB)),
            dma((2, CB)),
        ],
        compiler_params=pltpu.CompilerParams(
            collective_id=0, has_side_effects=True, vmem_limit_bytes=48 * 1024 * 1024
        ),
        cost_estimate=pl.CostEstimate(
            flops=2 * height * entries * tile * tile * width,
            bytes_accessed=2 * a_tiles.size,
            transcendentals=0,
        ),
    )(*(pltpu.with_memory_space_constraint(x, pltpu.HBM) for x in operands))


def solution(mesh):
    in_specs = (
        P("row", None, None, None),
        P("row", None),
        P("row", "col", None, None),
        P("row", "col"),
        P("row", None),
    )
    out_specs = P("row", "col", None, None)
    return jax.shard_map(shards, mesh=mesh, in_specs=in_specs, out_specs=out_specs, check_vma=False)
```

```python
import functools

import jax
import jax.numpy as jnp
from jax import lax
from jax.experimental import pallas as pl
from jax.experimental.pallas import tpu as pltpu
from jax.sharding import PartitionSpec as P

CB = 2
SPAN = 3
PARTS = 4
MESH = pl.DeviceIdType.MESH


def wrap(value, size):
    return jnp.where(value < 0, value + size, value)


def kernel(
    rows,
    a_cols_ref,
    p_cols_ref,
    send_rows_ref,
    p_hbm,
    a_ref,
    out_ref,
    a_cols,
    p_cols,
    send_rows,
    p_ref,
    a_buf,
    ghost_out,
    ghost_out_ids,
    ghost_in,
    ghost_in_ids,
    slots,
    marks,
    blocks,
    running,
    padded,
    table_v,
    table,
    grouped,
    part_out,
    part_in,
    small_sem,
    table_sem,
    a_sem,
    ghost_send,
    ghost_recv,
    slot_send,
    slot_recv,
    mark_send,
    mark_recv,
    part_send,
    part_recv,
):
    height, entries, tile = a_buf.shape[0], a_buf.shape[1], a_buf.shape[2]
    capacity = ghost_out.shape[1]
    coarse = CB * rows
    column_count = out_ref.shape[1]
    per_part = height // PARTS
    zero_block = height + 2 * capacity
    pairs = (entries + SPAN) // 2
    s = lax.axis_index("row")
    k = lax.axis_index("col")
    after, before = lax.rem(s + 1, rows), lax.rem(s + rows - 1, rows)
    mate = k + 1 - 2 * lax.rem(k, 2)
    across = lax.rem(k + 2, 4)
    odd = lax.rem(k, 2)
    late = 1 - lax.rem(k // 2 + s, 2)

    barrier = pltpu.get_barrier_semaphore()
    for device in ({"row": before}, {"row": after}, {"col": mate}, {"col": across}):
        pl.semaphore_signal(barrier, inc=1, device_id=device, device_id_type=MESH)

    small = [
        pltpu.make_async_copy(source, target, small_sem.at[n])
        for n, (source, target) in enumerate(
            (
                (p_hbm, p_ref),
                (send_rows_ref, send_rows),
                (p_cols_ref, p_cols),
                (a_cols_ref, a_cols),
            )
        )
    ]
    for copy in small:
        copy.start()

    def a_copy(i):
        return pltpu.make_async_copy(a_ref.at[i], a_buf.at[i], a_sem.at[i])

    def start_a(i, carry):
        a_copy(i).start()
        return carry

    def wait_a(i, carry):
        a_copy(i).wait()
        return carry

    lax.fori_loop(0, height // 2, start_a, 0)

    def first_id(slab):
        return lax.rem(CB * slab + coarse - 4, coarse)

    def first_column(slab):
        start = first_id(slab)
        offset = lax.rem(k + 4 - lax.rem(start, 4), 4)
        return lax.rem((start + offset) // 4, column_count)

    def place_group(place):
        return jnp.where(place >= 4, 1, 0) + jnp.where(place >= 8, 1, 0)

    start = first_id(s)
    left_start = lax.rem(CB * s + coarse - 2, coarse)
    for copy in small:
        copy.wait()

    for side in range(2):
        for t in range(capacity):
            row = send_rows[side, t]
            ghost_out[side, t] = p_ref[row, 0]
            ghost_out_ids[side, t : t + 1] = jnp.full((1, tile), p_cols[row], jnp.int32)
    padded[...] = jnp.zeros_like(padded)
    padded[:, :entries] = a_cols[...]
    listed = padded[...]

    def own_part(part, group):
        for n in range(per_part):
            i = part * per_part + n
            block = p_ref[i, 0]
            blocks[i] = block
            slots[0, part, :, n * tile : (n + 1) * tile] = block.T
            place = wrap(p_cols[i] - left_start, coarse)
            marks[0, pl.ds(i, 1)] = jnp.full((1, tile), jnp.where(place >= 4, 1.0, 0.0), jnp.float32)
            group = group + jnp.where(listed == i, place_group(wrap(p_cols[i] - start, coarse)), 0)
        return group

    group = lax.fori_loop(0, PARTS, own_part, jnp.zeros_like(listed))

    pl.semaphore_wait(barrier, 4)

    def ghost_copies(side):
        target = {"row": after if side == 0 else before}
        return [
            pltpu.make_async_remote_copy(
                src_ref=src.at[side],
                dst_ref=dst.at[side],
                send_sem=ghost_send.at[side, n],
                recv_sem=ghost_recv.at[side, n],
                device_id=target,
                device_id_type=MESH,
            )
            for n, (src, dst) in enumerate(((ghost_out, ghost_in), (ghost_out_ids, ghost_in_ids)))
        ]

    hops = {1: (0, mate), 2: (0, across), 3: (2, mate)}

    def slot_copy(hop, part):
        source, target = hops[hop]
        return pltpu.make_async_remote_copy(
            src_ref=slots.at[source, part],
            dst_ref=slots.at[hop, part],
            send_sem=slot_send.at[hop - 1, part],
            recv_sem=slot_recv.at[hop - 1, part],
            device_id={"col": target},
            device_id_type=MESH,
        )

    def mark_copy(hop):
        source, target = hops[hop]
        return pltpu.make_async_remote_copy(
            src_ref=marks.at[source],
            dst_ref=marks.at[hop],
            send_sem=mark_send.at[hop - 1],
            recv_sem=mark_recv.at[hop - 1],
            device_id={"col": target},
            device_id_type=MESH,
        )

    def send_slot(hop):
        mark_copy(hop).start()
        for part in range(PARTS):
            slot_copy(hop, part).start()

    def receive_slot(hop):
        mark_copy(hop).wait_recv()
        for part in range(PARTS):
            slot_copy(hop, part).wait_recv()

    def forward(part):
        slot_copy(2, part).wait_recv()
        slot_copy(3, part).start()

    def forward_mark():
        mark_copy(2).wait_recv()
        mark_copy(3).start()

    for side in range(2):
        for copy in ghost_copies(side):
            copy.start()

    @pl.when(odd == 0)
    def _():
        send_slot(2)

    send_slot(1)
    lax.fori_loop(height // 2, height, start_a, 0)

    blocks[zero_block] = jnp.zeros((tile, tile), jnp.bfloat16)
    running[pairs] = jnp.zeros((tile, tile), jnp.float32)

    def clear(c, carry):
        for r in range(CB):
            out_ref[r, c] = jnp.zeros((tile, tile), jnp.float32)
        return carry

    lax.fori_loop(0, column_count, clear, 0)

    for side in range(2):
        for copy in ghost_copies(side):
            copy.wait_recv()
        for t in range(capacity):
            j = height + side * capacity + t
            blocks[j] = ghost_in[side, t]
            place = wrap(ghost_in_ids[side, t : t + 1] - start, coarse)
            group = group + jnp.where(listed == j, place_group(place), 0)

    @pl.when(odd == 1)
    def _():
        send_slot(2)

    lane = lax.broadcasted_iota(jnp.int32, listed.shape, 1)
    byte = jnp.where(group == 0, 1, jnp.where(group == 1, 1 << 8, 1 << 16))
    scan = jnp.where(lane < entries, byte, 0)
    step = 1
    while step < entries:
        scan = scan + jnp.where(lane >= step, pltpu.roll(scan, step, 1), 0)
        step *= 2
    total_counts = scan[:, entries - 1 : entries]
    counts = [(total_counts >> (8 * g)) & 255 for g in range(SPAN)]
    sizes = [((c + 1) >> 1) << 1 for c in counts]
    starts = [jnp.zeros_like(sizes[0]), sizes[0], sizes[0] + sizes[1]]
    slot = jnp.zeros_like(listed)
    for g in range(SPAN):
        slot = slot + jnp.where(group == g, starts[g] + ((scan >> (8 * g)) & 255) - 1, 0)
    packed = jnp.zeros_like(listed)
    for m in range(entries):
        packed = packed + jnp.where(
            slot[:, m : m + 1] == lane, (listed[:, m : m + 1] - zero_block) * 32 + m, 0
        )
    chosen = packed & 31
    column = (packed >> 5) + zero_block
    facts = jnp.ones_like(listed)
    for g in range(SPAN):
        facts = jnp.where(2 * lane == starts[g], 0, facts)
    for g in range(SPAN):
        last = jnp.where(counts[g] > 0, ((starts[g] + sizes[g]) >> 1) - 1, pairs)
        facts = jnp.where(lane == 16 + g, last, facts)
    table_v[...] = jnp.where(
        lane < 32,
        chosen,
        jnp.where(lane < 64, pltpu.roll(column, 32, 1), pltpu.roll(facts, 64, 1)),
    )
    table_copy = pltpu.make_async_copy(table_v, table, table_sem)
    table_copy.start()
    table_copy.wait()
    lax.fori_loop(0, height, wait_a, 0)

    def multiply(i, carry):
        total = None
        for pair in range(pairs):
            at = (2 * pair, 2 * pair + 1)
            left = jnp.concatenate([a_buf[i, table[i, n]] for n in at], axis=1)
            right = jnp.concatenate([blocks[table[i, 32 + n]] for n in at], axis=0)
            term = jnp.dot(left, right, preferred_element_type=jnp.float32)
            total = term if pair == 0 else jnp.where(table[i, 64 + pair] > 0, total, 0.0) + term
            running[pair] = total
        rows_of = pl.ds(pl.multiple_of(i * tile, tile), tile)
        for g in range(SPAN):
            grouped[rows_of, g * tile : (g + 1) * tile] = running[table[i, 80 + g]].astype(jnp.bfloat16)

        @pl.when((odd == 0) & (i == height // 2))
        def _():
            forward_mark()
            forward(0)
            forward(1)

        @pl.when((odd == 0) & (i == height * 3 // 4))
        def _():
            forward(2)
            forward(3)

        return carry

    lax.fori_loop(0, height, multiply, 0)

    own_column = first_column(s)

    def part_copy(side, o, wide):
        columns = pl.ds(SPAN - 1, 1) if wide else pl.ds(0, SPAN - 1)
        return pltpu.make_async_remote_copy(
            src_ref=part_out.at[side, o, columns],
            dst_ref=part_in.at[side, o, columns],
            send_sem=part_send.at[side, o, wide],
            recv_sem=part_recv.at[side, o, wide],
            device_id={"row": before if side == 0 else after},
            device_id_type=MESH,
        )

    @pl.when(odd == 1)
    def _():
        forward_mark()
        for part in range(PARTS - 1):
            forward(part)

    receive_slot(1)

    def use_slot(step, carry):
        second = lax.rem(step, 2)
        others = step == 2 * (1 - late) + second

        @pl.when(others & (odd + second == 1))
        def _():
            receive_slot(3)

        @pl.when(others & (odd == 1) & (second == 1))
        def _():
            forward(PARTS - 1)

        index = lax.rem(2 * late + 2 * (step // 2), 4) + odd + second - 2 * odd * second
        total = None
        for part in range(PARTS):
            left = slots[index, part]
            mark = jnp.concatenate(
                [marks[index, part * per_part + n : part * per_part + n + 1] for n in range(per_part)],
                axis=1,
            )
            high = (left.astype(jnp.float32) * mark).astype(jnp.bfloat16)
            left = jnp.concatenate([left - high, high], axis=0)
            depth = per_part * tile
            term = jnp.dot(
                left, grouped[part * depth : (part + 1) * depth], preferred_element_type=jnp.float32
            )
            total = term if total is None else total + term

        @pl.when(step < 2)
        def _():
            for g in range(SPAN):
                columns = slice(g * tile, (g + 1) * tile)
                part_out[0, second, g] = total[:tile, columns].astype(jnp.bfloat16)
                part_out[1, second, g] = total[tile:, columns].astype(jnp.bfloat16)
            for side in range(2):
                part_copy(side, second, 0).start()

            @pl.when(late == 1)
            def _():
                for side in range(2):
                    part_copy(side, second, 1).start()

        @pl.when(step >= 2)
        def _():
            for g in range(SPAN):
                out_ref[second, lax.rem(own_column + g, column_count)] = total[
                    :tile, g * tile : (g + 1) * tile
                ]

        return carry

    lax.fori_loop(0, 4, use_slot, 0)

    columns_in = [first_column(after), first_column(before)]

    def collect(o, carry):
        for side in range(2):

            def add(g):
                at = lax.rem(columns_in[side] + g, column_count)
                out_ref[o, at] = out_ref[o, at] + part_in[side, o, g].astype(jnp.float32)

            part_copy(side, o, 0).wait_recv()
            for g in range(SPAN - 1):
                add(g)

            @pl.when(late == 0)
            def _():
                part_copy(side, o, 1).wait_recv()
                add(SPAN - 1)

        return carry

    lax.fori_loop(0, CB, collect, 0)

    for side in range(2):
        for copy in ghost_copies(side):
            copy.wait_send()
        for o in range(CB):
            part_copy(side, o, 0).wait_send()

    @pl.when(late == 1)
    def _():
        for side in range(2):
            for o in range(CB):
                part_copy(side, o, 1).wait_send()

    for hop in (1, 2, 3):
        mark_copy(hop).wait_send()
        for part in range(PARTS):
            slot_copy(hop, part).wait_send()


def shards(a_tiles, a_cols, p_tiles, p_cols, send_rows):
    rows, cols = lax.axis_size("row"), lax.axis_size("col")
    assert cols == 4
    height, entries, tile, _ = a_tiles.shape
    capacity = send_rows.shape[1]
    column_count = CB * rows // cols
    width = SPAN * tile
    vmem = pl.BlockSpec(memory_space=pltpu.VMEM)
    operands = (a_cols, p_cols.reshape(height), send_rows, p_tiles, a_tiles)
    bf16, f32, i32 = jnp.bfloat16, jnp.float32, jnp.int32
    dma = pltpu.SemaphoreType.DMA
    return pl.pallas_call(
        functools.partial(kernel, rows),
        out_shape=jax.ShapeDtypeStruct((CB, column_count, tile, tile), f32),
        in_specs=[pl.BlockSpec(memory_space=pltpu.HBM)] * 5,
        out_specs=vmem,
        scratch_shapes=[
            pltpu.VMEM(a_cols.shape, i32),
            pltpu.SMEM((height,), i32),
            pltpu.SMEM(send_rows.shape, i32),
            pltpu.VMEM(p_tiles.shape, bf16),
            pltpu.VMEM(a_tiles.shape, bf16),
            pltpu.VMEM((2, capacity, tile, tile), bf16),
            pltpu.VMEM((2, 8, tile), i32),
            pltpu.VMEM((2, capacity, tile, tile), bf16),
            pltpu.VMEM((2, 8, tile), i32),
            pltpu.VMEM((4, PARTS, tile, height // PARTS * tile), bf16),
            pltpu.VMEM((4, height, tile), f32),
            pltpu.VMEM((height + 2 * capacity + 1, tile, tile), bf16),
            pltpu.VMEM(((entries + SPAN) // 2 + 1, tile, tile), f32),
            pltpu.VMEM((height, 128), i32),
            pltpu.VMEM((height, 128), i32),
            pltpu.SMEM((height, 128), i32),
            pltpu.VMEM((height * tile, width), bf16),
            pltpu.VMEM((2, CB, SPAN, tile, tile), bf16),
            pltpu.VMEM((2, CB, SPAN, tile, tile), bf16),
            dma((4,)),
            dma,
            dma((height,)),
            dma((2, 2)),
            dma((2, 2)),
            dma((3, PARTS)),
            dma((3, PARTS)),
            dma((3,)),
            dma((3,)),
            dma((2, CB, 2)),
            dma((2, CB, 2)),
        ],
        compiler_params=pltpu.CompilerParams(
            collective_id=0, has_side_effects=True, vmem_limit_bytes=48 * 1024 * 1024
        ),
        cost_estimate=pl.CostEstimate(
            flops=2 * height * entries * tile * tile * width,
            bytes_accessed=2 * a_tiles.size,
            transcendentals=0,
        ),
    )(*(pltpu.with_memory_space_constraint(x, pltpu.HBM) for x in operands))


def solution(mesh):
    in_specs = (
        P("row", None, None, None),
        P("row", None),
        P("row", "col", None, None),
        P("row", "col"),
        P("row", None),
    )
    out_specs = P("row", "col", None, None)
    return jax.shard_map(shards, mesh=mesh, in_specs=in_specs, out_specs=out_specs, check_vma=False)
```

```python
import functools

import jax
import jax.numpy as jnp
from jax import lax
from jax.experimental import pallas as pl
from jax.experimental.pallas import tpu as pltpu
from jax.sharding import PartitionSpec as P

CB = 2
SPAN = 3
PARTS = 4
MESH = pl.DeviceIdType.MESH


def wrap(value, size):
    return jnp.where(value < 0, value + size, value)


def kernel(
    rows,
    a_cols_ref,
    p_cols_ref,
    send_rows_ref,
    p_hbm,
    a_ref,
    out_ref,
    a_cols,
    p_cols,
    send_rows,
    p_ref,
    a_buf,
    ghost_out,
    ghost_out_ids,
    ghost_in,
    ghost_in_ids,
    slots,
    marks,
    blocks,
    running_even,
    running_odd,
    padded,
    table_v,
    table,
    grouped,
    part_out,
    part_in,
    small_sem,
    table_sem,
    a_sem,
    ghost_send,
    ghost_recv,
    slot_send,
    slot_recv,
    mark_send,
    mark_recv,
    part_send,
    part_recv,
):
    height, entries, tile = a_buf.shape[0], a_buf.shape[1], a_buf.shape[2]
    capacity = ghost_out.shape[1]
    coarse = CB * rows
    column_count = out_ref.shape[1]
    per_part = height // PARTS
    zero_block = height + 2 * capacity
    pairs = (entries + SPAN) // 2
    s = lax.axis_index("row")
    k = lax.axis_index("col")
    after, before = lax.rem(s + 1, rows), lax.rem(s + rows - 1, rows)
    mate = k + 1 - 2 * lax.rem(k, 2)
    across = lax.rem(k + 2, 4)
    odd = lax.rem(k, 2)
    late = 1 - lax.rem(k // 2 + s, 2)

    barrier = pltpu.get_barrier_semaphore()
    for device in ({"row": before}, {"row": after}, {"col": mate}, {"col": across}):
        pl.semaphore_signal(barrier, inc=1, device_id=device, device_id_type=MESH)

    small = [
        pltpu.make_async_copy(source, target, small_sem.at[n])
        for n, (source, target) in enumerate(
            (
                (p_hbm, p_ref),
                (send_rows_ref, send_rows),
                (p_cols_ref, p_cols),
                (a_cols_ref, a_cols),
            )
        )
    ]
    for copy in small:
        copy.start()

    def a_copy(i):
        return pltpu.make_async_copy(a_ref.at[i], a_buf.at[i], a_sem.at[i])

    def start_a(i, carry):
        a_copy(i).start()
        return carry

    def wait_a(i, carry):
        a_copy(i).wait()
        return carry

    lax.fori_loop(0, height // 2, start_a, 0)

    def first_id(slab):
        return lax.rem(CB * slab + coarse - 4, coarse)

    def first_column(slab):
        start = first_id(slab)
        offset = lax.rem(k + 4 - lax.rem(start, 4), 4)
        return lax.rem((start + offset) // 4, column_count)

    def place_group(place):
        return jnp.where(place >= 4, 1, 0) + jnp.where(place >= 8, 1, 0)

    start = first_id(s)
    left_start = lax.rem(CB * s + coarse - 2, coarse)
    for copy in small:
        copy.wait()

    for side in range(2):
        for t in range(capacity):
            row = send_rows[side, t]
            ghost_out[side, t] = p_ref[row, 0]
            ghost_out_ids[side, t : t + 1] = jnp.full((1, tile), p_cols[row], jnp.int32)
    padded[...] = jnp.zeros_like(padded)
    padded[:, :entries] = a_cols[...]
    listed = padded[...]

    pl.semaphore_wait(barrier, 4)

    def ghost_copies(side):
        target = {"row": after if side == 0 else before}
        return [
            pltpu.make_async_remote_copy(
                src_ref=src.at[side],
                dst_ref=dst.at[side],
                send_sem=ghost_send.at[side, n],
                recv_sem=ghost_recv.at[side, n],
                device_id=target,
                device_id_type=MESH,
            )
            for n, (src, dst) in enumerate(((ghost_out, ghost_in), (ghost_out_ids, ghost_in_ids)))
        ]

    hops = {1: (0, mate), 2: (0, across), 3: (2, mate)}

    def slot_copy(hop, part):
        source, target = hops[hop]
        return pltpu.make_async_remote_copy(
            src_ref=slots.at[source, part],
            dst_ref=slots.at[hop, part],
            send_sem=slot_send.at[hop - 1, part],
            recv_sem=slot_recv.at[hop - 1, part],
            device_id={"col": target},
            device_id_type=MESH,
        )

    def mark_copy(hop):
        source, target = hops[hop]
        return pltpu.make_async_remote_copy(
            src_ref=marks.at[source],
            dst_ref=marks.at[hop],
            send_sem=mark_send.at[hop - 1],
            recv_sem=mark_recv.at[hop - 1],
            device_id={"col": target},
            device_id_type=MESH,
        )

    def send_slot(hop):
        mark_copy(hop).start()
        for part in range(PARTS):
            slot_copy(hop, part).start()

    def receive_slot(hop):
        mark_copy(hop).wait_recv()
        for part in range(PARTS):
            slot_copy(hop, part).wait_recv()

    def forward(part):
        slot_copy(2, part).wait_recv()
        slot_copy(3, part).start()

    def forward_mark():
        mark_copy(2).wait_recv()
        mark_copy(3).start()

    for side in range(2):
        for copy in ghost_copies(side):
            copy.start()

    def own_part(part, group):
        for n in range(per_part):
            i = part * per_part + n
            block = p_ref[i, 0]
            blocks[i] = block
            slots[0, part, :, n * tile : (n + 1) * tile] = block.T
            place = wrap(p_cols[i] - left_start, coarse)
            marks[0, pl.ds(i, 1)] = jnp.full((1, tile), jnp.where(place >= 4, 1.0, 0.0), jnp.float32)
            group = group + jnp.where(listed == i, place_group(wrap(p_cols[i] - start, coarse)), 0)

        @pl.when(odd == 0)
        def _():
            slot_copy(2, part).start()

        slot_copy(1, part).start()
        return group

    group = lax.fori_loop(0, PARTS, own_part, jnp.zeros_like(listed))

    mark_copy(1).start()

    @pl.when(odd == 0)
    def _():
        mark_copy(2).start()

    lax.fori_loop(height // 2, height, start_a, 0)

    blocks[zero_block] = jnp.zeros((tile, tile), jnp.bfloat16)
    for running in (running_even, running_odd):
        running[pairs] = jnp.zeros((tile, tile), jnp.float32)

    def clear(c, carry):
        for r in range(CB):
            out_ref[r, c] = jnp.zeros((tile, tile), jnp.float32)
        return carry

    lax.fori_loop(0, column_count, clear, 0)

    for side in range(2):
        for copy in ghost_copies(side):
            copy.wait_recv()
        for t in range(capacity):
            j = height + side * capacity + t
            blocks[j] = ghost_in[side, t]
            place = wrap(ghost_in_ids[side, t : t + 1] - start, coarse)
            group = group + jnp.where(listed == j, place_group(place), 0)

    @pl.when(odd == 1)
    def _():
        send_slot(2)

    lane = lax.broadcasted_iota(jnp.int32, listed.shape, 1)
    byte = jnp.where(group == 0, 1, jnp.where(group == 1, 1 << 8, 1 << 16))
    scan = jnp.where(lane < entries, byte, 0)
    step = 1
    while step < entries:
        scan = scan + jnp.where(lane >= step, pltpu.roll(scan, step, 1), 0)
        step *= 2
    total_counts = scan[:, entries - 1 : entries]
    counts = [(total_counts >> (8 * g)) & 255 for g in range(SPAN)]
    sizes = [((c + 1) >> 1) << 1 for c in counts]
    starts = [jnp.zeros_like(sizes[0]), sizes[0], sizes[0] + sizes[1]]
    slot = jnp.zeros_like(listed)
    for g in range(SPAN):
        slot = slot + jnp.where(group == g, starts[g] + ((scan >> (8 * g)) & 255) - 1, 0)
    packed = jnp.zeros_like(listed)
    for m in range(entries):
        packed = packed + jnp.where(
            slot[:, m : m + 1] == lane, (listed[:, m : m + 1] - zero_block) * 32 + m, 0
        )
    chosen = packed & 31
    column = (packed >> 5) + zero_block
    facts = jnp.ones_like(listed)
    for g in range(SPAN):
        facts = jnp.where(2 * lane == starts[g], 0, facts)
    for g in range(SPAN):
        last = jnp.where(counts[g] > 0, ((starts[g] + sizes[g]) >> 1) - 1, pairs)
        facts = jnp.where(lane == 16 + g, last, facts)
    table_v[...] = jnp.where(
        lane < 32,
        chosen,
        jnp.where(lane < 64, pltpu.roll(column, 32, 1), pltpu.roll(facts, 64, 1)),
    )
    table_copy = pltpu.make_async_copy(table_v, table, table_sem)
    table_copy.start()
    table_copy.wait()
    lax.fori_loop(0, height, wait_a, 0)

    def group_row(i, running):
        total = None
        for pair in range(pairs):
            at = (2 * pair, 2 * pair + 1)
            left = jnp.concatenate([a_buf[i, table[i, n]] for n in at], axis=1)
            right = jnp.concatenate([blocks[table[i, 32 + n]] for n in at], axis=0)
            term = jnp.dot(left, right, preferred_element_type=jnp.float32)
            total = term if pair == 0 else jnp.where(table[i, 64 + pair] > 0, total, 0.0) + term
            running[pair] = total
        rows_of = pl.ds(pl.multiple_of(i * tile, tile), tile)
        for g in range(SPAN):
            grouped[rows_of, g * tile : (g + 1) * tile] = running[table[i, 80 + g]].astype(jnp.bfloat16)

    def multiply(both, carry):
        i = 2 * both
        group_row(i, running_even)
        group_row(i + 1, running_odd)

        @pl.when((odd == 0) & (i == height // 2))
        def _():
            forward_mark()
            forward(0)
            forward(1)

        @pl.when((odd == 0) & (i == height * 3 // 4))
        def _():
            forward(2)
            forward(3)

        return carry

    lax.fori_loop(0, height // 2, multiply, 0)

    own_column = first_column(s)

    def part_copy(side, o, wide):
        columns = pl.ds(SPAN - 1, 1) if wide else pl.ds(0, SPAN - 1)
        return pltpu.make_async_remote_copy(
            src_ref=part_out.at[side, o, columns],
            dst_ref=part_in.at[side, o, columns],
            send_sem=part_send.at[side, o, wide],
            recv_sem=part_recv.at[side, o, wide],
            device_id={"row": before if side == 0 else after},
            device_id_type=MESH,
        )

    @pl.when(odd == 1)
    def _():
        forward_mark()
        for part in range(PARTS - 1):
            forward(part)

    receive_slot(1)

    def use_slot(step, carry):
        second = lax.rem(step, 2)
        others = step == 2 * (1 - late) + second

        @pl.when(others & (odd + second == 1))
        def _():
            receive_slot(3)

        @pl.when(others & (odd == 1) & (second == 1))
        def _():
            forward(PARTS - 1)

        index = lax.rem(2 * late + 2 * (step // 2), 4) + odd + second - 2 * odd * second
        total = None
        for part in range(PARTS):
            left = slots[index, part]
            mark = jnp.concatenate(
                [marks[index, part * per_part + n : part * per_part + n + 1] for n in range(per_part)],
                axis=1,
            )
            high = (left.astype(jnp.float32) * mark).astype(jnp.bfloat16)
            left = jnp.concatenate([left - high, high], axis=0)
            depth = per_part * tile
            term = jnp.dot(
                left, grouped[part * depth : (part + 1) * depth], preferred_element_type=jnp.float32
            )
            total = term if total is None else total + term

        @pl.when(step < 2)
        def _():
            for g in range(SPAN):
                columns = slice(g * tile, (g + 1) * tile)
                part_out[0, second, g] = total[:tile, columns].astype(jnp.bfloat16)
                part_out[1, second, g] = total[tile:, columns].astype(jnp.bfloat16)
            for side in range(2):
                part_copy(side, second, 0).start()

            @pl.when(late == 1)
            def _():
                for side in range(2):
                    part_copy(side, second, 1).start()

        @pl.when(step >= 2)
        def _():
            for g in range(SPAN):
                out_ref[second, lax.rem(own_column + g, column_count)] = total[
                    :tile, g * tile : (g + 1) * tile
                ]

        return carry

    lax.fori_loop(0, 4, use_slot, 0)

    columns_in = [first_column(after), first_column(before)]

    def collect(o, carry):
        for side in range(2):

            def add(g):
                at = lax.rem(columns_in[side] + g, column_count)
                out_ref[o, at] = out_ref[o, at] + part_in[side, o, g].astype(jnp.float32)

            part_copy(side, o, 0).wait_recv()
            for g in range(SPAN - 1):
                add(g)

            @pl.when(late == 0)
            def _():
                part_copy(side, o, 1).wait_recv()
                add(SPAN - 1)

        return carry

    lax.fori_loop(0, CB, collect, 0)

    for side in range(2):
        for copy in ghost_copies(side):
            copy.wait_send()
        for o in range(CB):
            part_copy(side, o, 0).wait_send()

    @pl.when(late == 1)
    def _():
        for side in range(2):
            for o in range(CB):
                part_copy(side, o, 1).wait_send()

    for hop in (1, 2, 3):
        mark_copy(hop).wait_send()
        for part in range(PARTS):
            slot_copy(hop, part).wait_send()


def shards(a_tiles, a_cols, p_tiles, p_cols, send_rows):
    rows, cols = lax.axis_size("row"), lax.axis_size("col")
    assert cols == 4
    height, entries, tile, _ = a_tiles.shape
    capacity = send_rows.shape[1]
    column_count = CB * rows // cols
    width = SPAN * tile
    vmem = pl.BlockSpec(memory_space=pltpu.VMEM)
    operands = (a_cols, p_cols.reshape(height), send_rows, p_tiles, a_tiles)
    bf16, f32, i32 = jnp.bfloat16, jnp.float32, jnp.int32
    dma = pltpu.SemaphoreType.DMA
    return pl.pallas_call(
        functools.partial(kernel, rows),
        out_shape=jax.ShapeDtypeStruct((CB, column_count, tile, tile), f32),
        in_specs=[pl.BlockSpec(memory_space=pltpu.HBM)] * 5,
        out_specs=vmem,
        scratch_shapes=[
            pltpu.VMEM(a_cols.shape, i32),
            pltpu.SMEM((height,), i32),
            pltpu.SMEM(send_rows.shape, i32),
            pltpu.VMEM(p_tiles.shape, bf16),
            pltpu.VMEM(a_tiles.shape, bf16),
            pltpu.VMEM((2, capacity, tile, tile), bf16),
            pltpu.VMEM((2, 8, tile), i32),
            pltpu.VMEM((2, capacity, tile, tile), bf16),
            pltpu.VMEM((2, 8, tile), i32),
            pltpu.VMEM((4, PARTS, tile, height // PARTS * tile), bf16),
            pltpu.VMEM((4, height, tile), f32),
            pltpu.VMEM((height + 2 * capacity + 1, tile, tile), bf16),
            pltpu.VMEM(((entries + SPAN) // 2 + 1, tile, tile), f32),
            pltpu.VMEM(((entries + SPAN) // 2 + 1, tile, tile), f32),
            pltpu.VMEM((height, 128), i32),
            pltpu.VMEM((height, 128), i32),
            pltpu.SMEM((height, 128), i32),
            pltpu.VMEM((height * tile, width), bf16),
            pltpu.VMEM((2, CB, SPAN, tile, tile), bf16),
            pltpu.VMEM((2, CB, SPAN, tile, tile), bf16),
            dma((4,)),
            dma,
            dma((height,)),
            dma((2, 2)),
            dma((2, 2)),
            dma((3, PARTS)),
            dma((3, PARTS)),
            dma((3,)),
            dma((3,)),
            dma((2, CB, 2)),
            dma((2, CB, 2)),
        ],
        compiler_params=pltpu.CompilerParams(
            collective_id=0, has_side_effects=True, vmem_limit_bytes=48 * 1024 * 1024
        ),
        cost_estimate=pl.CostEstimate(
            flops=2 * height * entries * tile * tile * width,
            bytes_accessed=2 * a_tiles.size,
            transcendentals=0,
        ),
    )(*(pltpu.with_memory_space_constraint(x, pltpu.HBM) for x in operands))


def solution(mesh):
    in_specs = (
        P("row", None, None, None),
        P("row", None),
        P("row", "col", None, None),
        P("row", "col"),
        P("row", None),
    )
    out_specs = P("row", "col", None, None)
    return jax.shard_map(shards, mesh=mesh, in_specs=in_specs, out_specs=out_specs, check_vma=False)
```

```python
import functools

import jax
import jax.numpy as jnp
from jax import lax
from jax.experimental import pallas as pl
from jax.experimental.pallas import tpu as pltpu
from jax.sharding import PartitionSpec as P

CB = 2
SPAN = 3
PARTS = 4
MESH = pl.DeviceIdType.MESH


def wrap(value, size):
    return jnp.where(value < 0, value + size, value)


def kernel(
    rows,
    a_cols_ref,
    p_cols_ref,
    send_rows_ref,
    p_hbm,
    a_ref,
    out_ref,
    a_cols,
    p_cols,
    send_rows,
    p_ref,
    a_buf,
    ghost_out,
    ghost_out_ids,
    ghost_in,
    ghost_in_ids,
    slots,
    marks,
    blocks,
    running_even,
    running_odd,
    padded,
    table_v,
    table,
    grouped,
    part_out,
    part_in,
    small_sem,
    table_sem,
    a_sem,
    ghost_send,
    ghost_recv,
    slot_send,
    slot_recv,
    mark_send,
    mark_recv,
    part_send,
    part_recv,
):
    height, entries, tile = a_buf.shape[0], a_buf.shape[1], a_buf.shape[2]
    capacity = ghost_out.shape[1]
    coarse = CB * rows
    column_count = out_ref.shape[1]
    per_part = height // PARTS
    zero_block = height + 2 * capacity
    pairs = (entries + SPAN) // 2
    s = lax.axis_index("row")
    k = lax.axis_index("col")
    after, before = lax.rem(s + 1, rows), lax.rem(s + rows - 1, rows)
    mate = k + 1 - 2 * lax.rem(k, 2)
    across = lax.rem(k + 2, 4)
    odd = lax.rem(k, 2)
    late = 1 - lax.rem(k // 2 + s, 2)

    barrier = pltpu.get_barrier_semaphore()
    for device in ({"row": before}, {"row": after}, {"col": mate}, {"col": across}):
        pl.semaphore_signal(barrier, inc=1, device_id=device, device_id_type=MESH)

    small = [
        pltpu.make_async_copy(source, target, small_sem.at[n])
        for n, (source, target) in enumerate(
            (
                (p_hbm, p_ref),
                (send_rows_ref, send_rows),
                (p_cols_ref, p_cols),
                (a_cols_ref, a_cols),
            )
        )
    ]
    for copy in small:
        copy.start()

    def a_copy(i):
        return pltpu.make_async_copy(a_ref.at[i], a_buf.at[i], a_sem.at[i])

    def start_a(i, carry):
        a_copy(i).start()
        return carry

    def wait_a(i, carry):
        a_copy(i).wait()
        return carry

    lax.fori_loop(0, height // 2, start_a, 0)

    def first_id(slab):
        return lax.rem(CB * slab + coarse - 4, coarse)

    def first_column(slab):
        start = first_id(slab)
        offset = lax.rem(k + 4 - lax.rem(start, 4), 4)
        return lax.rem((start + offset) // 4, column_count)

    def place_group(place):
        return jnp.where(place >= 4, 1, 0) + jnp.where(place >= 8, 1, 0)

    start = first_id(s)
    left_start = lax.rem(CB * s + coarse - 2, coarse)
    for copy in small:
        copy.wait()

    for side in range(2):
        for t in range(capacity):
            row = send_rows[side, t]
            ghost_out[side, t] = p_ref[row, 0]
            ghost_out_ids[side, t : t + 1] = jnp.full((1, tile), p_cols[row], jnp.int32)
    padded[...] = jnp.zeros_like(padded)
    padded[:, :entries] = a_cols[...]
    listed = padded[...]

    pl.semaphore_wait(barrier, 4)

    def ghost_copies(side):
        target = {"row": after if side == 0 else before}
        return [
            pltpu.make_async_remote_copy(
                src_ref=src.at[side],
                dst_ref=dst.at[side],
                send_sem=ghost_send.at[side, n],
                recv_sem=ghost_recv.at[side, n],
                device_id=target,
                device_id_type=MESH,
            )
            for n, (src, dst) in enumerate(((ghost_out, ghost_in), (ghost_out_ids, ghost_in_ids)))
        ]

    hops = {1: (0, mate), 2: (0, across), 3: (2, mate)}

    def slot_copy(hop, part):
        source, target = hops[hop]
        return pltpu.make_async_remote_copy(
            src_ref=slots.at[source, part],
            dst_ref=slots.at[hop, part],
            send_sem=slot_send.at[hop - 1, part],
            recv_sem=slot_recv.at[hop - 1, part],
            device_id={"col": target},
            device_id_type=MESH,
        )

    def mark_copy(hop):
        source, target = hops[hop]
        return pltpu.make_async_remote_copy(
            src_ref=marks.at[source],
            dst_ref=marks.at[hop],
            send_sem=mark_send.at[hop - 1],
            recv_sem=mark_recv.at[hop - 1],
            device_id={"col": target},
            device_id_type=MESH,
        )

    def send_slot(hop):
        mark_copy(hop).start()
        for part in range(PARTS):
            slot_copy(hop, part).start()

    def receive_slot(hop):
        mark_copy(hop).wait_recv()
        for part in range(PARTS):
            slot_copy(hop, part).wait_recv()

    def forward(part):
        slot_copy(2, part).wait_recv()
        slot_copy(3, part).start()

    def forward_mark():
        mark_copy(2).wait_recv()
        mark_copy(3).start()

    for side in range(2):
        for copy in ghost_copies(side):
            copy.start()

    def own_part(part, group):
        for n in range(per_part):
            i = part * per_part + n
            block = p_ref[i, 0].T
            blocks[i] = block
            slots[0, part, :, n * tile : (n + 1) * tile] = block
            place = wrap(p_cols[i] - left_start, coarse)
            marks[0, pl.ds(i, 1)] = jnp.full((1, tile), jnp.where(place >= 4, 1.0, 0.0), jnp.float32)
            group = group + jnp.where(listed == i, place_group(wrap(p_cols[i] - start, coarse)), 0)

        @pl.when(odd == 0)
        def _():
            slot_copy(2, part).start()

        slot_copy(1, part).start()
        return group

    group = lax.fori_loop(0, PARTS, own_part, jnp.zeros_like(listed))

    mark_copy(1).start()

    @pl.when(odd == 0)
    def _():
        mark_copy(2).start()

    lax.fori_loop(height // 2, height, start_a, 0)

    blocks[zero_block] = jnp.zeros((tile, tile), jnp.bfloat16)
    for running in (running_even, running_odd):
        running[pairs] = jnp.zeros((tile, tile), jnp.float32)

    def clear(c, carry):
        for r in range(CB):
            out_ref[r, c] = jnp.zeros((tile, tile), jnp.float32)
        return carry

    lax.fori_loop(0, column_count, clear, 0)

    for side in range(2):
        for copy in ghost_copies(side):
            copy.wait_recv()
        for t in range(capacity):
            j = height + side * capacity + t
            blocks[j] = ghost_in[side, t].T
            place = wrap(ghost_in_ids[side, t : t + 1] - start, coarse)
            group = group + jnp.where(listed == j, place_group(place), 0)

    @pl.when(odd == 1)
    def _():
        send_slot(2)

    lane = lax.broadcasted_iota(jnp.int32, listed.shape, 1)
    byte = jnp.where(group == 0, 1, jnp.where(group == 1, 1 << 8, 1 << 16))
    scan = jnp.where(lane < entries, byte, 0)
    step = 1
    while step < entries:
        scan = scan + jnp.where(lane >= step, pltpu.roll(scan, step, 1), 0)
        step *= 2
    total_counts = scan[:, entries - 1 : entries]
    counts = [(total_counts >> (8 * g)) & 255 for g in range(SPAN)]
    sizes = [((c + 1) >> 1) << 1 for c in counts]
    starts = [jnp.zeros_like(sizes[0]), sizes[0], sizes[0] + sizes[1]]
    slot = jnp.zeros_like(listed)
    for g in range(SPAN):
        slot = slot + jnp.where(group == g, starts[g] + ((scan >> (8 * g)) & 255) - 1, 0)
    packed = jnp.zeros_like(listed)
    for m in range(entries):
        packed = packed + jnp.where(
            slot[:, m : m + 1] == lane, (listed[:, m : m + 1] - zero_block) * 32 + m, 0
        )
    chosen = packed & 31
    column = (packed >> 5) + zero_block
    facts = jnp.ones_like(listed)
    for g in range(SPAN):
        facts = jnp.where(2 * lane == starts[g], 0, facts)
    for g in range(SPAN):
        last = jnp.where(counts[g] > 0, ((starts[g] + sizes[g]) >> 1) - 1, pairs)
        facts = jnp.where(lane == 16 + g, last, facts)
    table_v[...] = jnp.where(
        lane < 32,
        chosen,
        jnp.where(lane < 64, pltpu.roll(column, 32, 1), pltpu.roll(facts, 64, 1)),
    )
    table_copy = pltpu.make_async_copy(table_v, table, table_sem)
    table_copy.start()
    table_copy.wait()
    lax.fori_loop(0, height, wait_a, 0)

    def group_row(i, running):
        total = None
        for pair in range(pairs):
            at = (2 * pair, 2 * pair + 1)
            left = jnp.concatenate([blocks[table[i, 32 + n]] for n in at], axis=1)
            right = jnp.concatenate([a_buf[i, table[i, n]] for n in at], axis=1)
            term = lax.dot_general(
                left, right, (((1,), (1,)), ((), ())), preferred_element_type=jnp.float32
            )
            total = term if pair == 0 else jnp.where(table[i, 64 + pair] > 0, total, 0.0) + term
            running[pair] = total
        rows_of = pl.ds(pl.multiple_of(i * tile, tile), tile)
        for g in range(SPAN):
            grouped[rows_of, g * tile : (g + 1) * tile] = running[table[i, 80 + g]].T.astype(jnp.bfloat16)

    def multiply(both, carry):
        i = 2 * both
        group_row(i, running_even)
        group_row(i + 1, running_odd)

        @pl.when((odd == 0) & (i == height // 2))
        def _():
            forward_mark()
            forward(0)
            forward(1)

        @pl.when((odd == 0) & (i == height * 3 // 4))
        def _():
            forward(2)
            forward(3)

        return carry

    lax.fori_loop(0, height // 2, multiply, 0)

    own_column = first_column(s)

    def part_copy(side, o, wide):
        columns = pl.ds(SPAN - 1, 1) if wide else pl.ds(0, SPAN - 1)
        return pltpu.make_async_remote_copy(
            src_ref=part_out.at[side, o, columns],
            dst_ref=part_in.at[side, o, columns],
            send_sem=part_send.at[side, o, wide],
            recv_sem=part_recv.at[side, o, wide],
            device_id={"row": before if side == 0 else after},
            device_id_type=MESH,
        )

    @pl.when(odd == 1)
    def _():
        forward_mark()
        for part in range(PARTS - 1):
            forward(part)

    receive_slot(1)

    def use_slot(step, carry):
        second = lax.rem(step, 2)
        others = step == 2 * (1 - late) + second

        @pl.when(others & (odd + second == 1))
        def _():
            receive_slot(3)

        @pl.when(others & (odd == 1) & (second == 1))
        def _():
            forward(PARTS - 1)

        index = lax.rem(2 * late + 2 * (step // 2), 4) + odd + second - 2 * odd * second
        total = None
        for part in range(PARTS):
            left = slots[index, part]
            mark = jnp.concatenate(
                [marks[index, part * per_part + n : part * per_part + n + 1] for n in range(per_part)],
                axis=1,
            )
            high = (left.astype(jnp.float32) * mark).astype(jnp.bfloat16)
            left = jnp.concatenate([left - high, high], axis=0)
            depth = per_part * tile
            term = jnp.dot(
                left, grouped[part * depth : (part + 1) * depth], preferred_element_type=jnp.float32
            )
            total = term if total is None else total + term

        @pl.when(step < 2)
        def _():
            for g in range(SPAN):
                columns = slice(g * tile, (g + 1) * tile)
                part_out[0, second, g] = total[:tile, columns].astype(jnp.bfloat16)
                part_out[1, second, g] = total[tile:, columns].astype(jnp.bfloat16)
            for side in range(2):
                part_copy(side, second, 0).start()

            @pl.when(late == 1)
            def _():
                for side in range(2):
                    part_copy(side, second, 1).start()

        @pl.when(step >= 2)
        def _():
            for g in range(SPAN):
                out_ref[second, lax.rem(own_column + g, column_count)] = total[
                    :tile, g * tile : (g + 1) * tile
                ]

        return carry

    lax.fori_loop(0, 4, use_slot, 0)

    columns_in = [first_column(after), first_column(before)]

    def collect(o, carry):
        for side in range(2):

            def add(g):
                at = lax.rem(columns_in[side] + g, column_count)
                out_ref[o, at] = out_ref[o, at] + part_in[side, o, g].astype(jnp.float32)

            part_copy(side, o, 0).wait_recv()
            for g in range(SPAN - 1):
                add(g)

            @pl.when(late == 0)
            def _():
                part_copy(side, o, 1).wait_recv()
                add(SPAN - 1)

        return carry

    lax.fori_loop(0, CB, collect, 0)

    for side in range(2):
        for copy in ghost_copies(side):
            copy.wait_send()
        for o in range(CB):
            part_copy(side, o, 0).wait_send()

    @pl.when(late == 1)
    def _():
        for side in range(2):
            for o in range(CB):
                part_copy(side, o, 1).wait_send()

    for hop in (1, 2, 3):
        mark_copy(hop).wait_send()
        for part in range(PARTS):
            slot_copy(hop, part).wait_send()


def shards(a_tiles, a_cols, p_tiles, p_cols, send_rows):
    rows, cols = lax.axis_size("row"), lax.axis_size("col")
    assert cols == 4
    height, entries, tile, _ = a_tiles.shape
    capacity = send_rows.shape[1]
    column_count = CB * rows // cols
    width = SPAN * tile
    vmem = pl.BlockSpec(memory_space=pltpu.VMEM)
    operands = (a_cols, p_cols.reshape(height), send_rows, p_tiles, a_tiles)
    bf16, f32, i32 = jnp.bfloat16, jnp.float32, jnp.int32
    dma = pltpu.SemaphoreType.DMA
    return pl.pallas_call(
        functools.partial(kernel, rows),
        out_shape=jax.ShapeDtypeStruct((CB, column_count, tile, tile), f32),
        in_specs=[pl.BlockSpec(memory_space=pltpu.HBM)] * 5,
        out_specs=vmem,
        scratch_shapes=[
            pltpu.VMEM(a_cols.shape, i32),
            pltpu.SMEM((height,), i32),
            pltpu.SMEM(send_rows.shape, i32),
            pltpu.VMEM(p_tiles.shape, bf16),
            pltpu.VMEM(a_tiles.shape, bf16),
            pltpu.VMEM((2, capacity, tile, tile), bf16),
            pltpu.VMEM((2, 8, tile), i32),
            pltpu.VMEM((2, capacity, tile, tile), bf16),
            pltpu.VMEM((2, 8, tile), i32),
            pltpu.VMEM((4, PARTS, tile, height // PARTS * tile), bf16),
            pltpu.VMEM((4, height, tile), f32),
            pltpu.VMEM((height + 2 * capacity + 1, tile, tile), bf16),
            pltpu.VMEM(((entries + SPAN) // 2 + 1, tile, tile), f32),
            pltpu.VMEM(((entries + SPAN) // 2 + 1, tile, tile), f32),
            pltpu.VMEM((height, 128), i32),
            pltpu.VMEM((height, 128), i32),
            pltpu.SMEM((height, 128), i32),
            pltpu.VMEM((height * tile, width), bf16),
            pltpu.VMEM((2, CB, SPAN, tile, tile), bf16),
            pltpu.VMEM((2, CB, SPAN, tile, tile), bf16),
            dma((4,)),
            dma,
            dma((height,)),
            dma((2, 2)),
            dma((2, 2)),
            dma((3, PARTS)),
            dma((3, PARTS)),
            dma((3,)),
            dma((3,)),
            dma((2, CB, 2)),
            dma((2, CB, 2)),
        ],
        compiler_params=pltpu.CompilerParams(
            collective_id=0, has_side_effects=True, vmem_limit_bytes=48 * 1024 * 1024
        ),
        cost_estimate=pl.CostEstimate(
            flops=2 * height * entries * tile * tile * width,
            bytes_accessed=2 * a_tiles.size,
            transcendentals=0,
        ),
    )(*(pltpu.with_memory_space_constraint(x, pltpu.HBM) for x in operands))


def solution(mesh):
    in_specs = (
        P("row", None, None, None),
        P("row", None),
        P("row", "col", None, None),
        P("row", "col"),
        P("row", None),
    )
    out_specs = P("row", "col", None, None)
    return jax.shard_map(shards, mesh=mesh, in_specs=in_specs, out_specs=out_specs, check_vma=False)
```

```python
import functools

import jax
import jax.numpy as jnp
from jax import lax
from jax.experimental import pallas as pl
from jax.experimental.pallas import tpu as pltpu
from jax.sharding import PartitionSpec as P

CB = 2
SPAN = 3
PARTS = 4
MESH = pl.DeviceIdType.MESH


def wrap(value, size):
    return jnp.where(value < 0, value + size, value)


def kernel(
    rows,
    a_cols_ref,
    p_cols_ref,
    send_rows_ref,
    p_hbm,
    a_ref,
    out_ref,
    a_cols,
    p_cols,
    send_rows,
    p_ref,
    a_low,
    a_high,
    ghost_out,
    ghost_out_ids,
    ghost_in,
    ghost_in_ids,
    slots,
    marks,
    blocks,
    running_even,
    running_odd,
    padded,
    table_v,
    table,
    grouped,
    part_out,
    part_in,
    small_sem,
    table_sem,
    a_sem,
    ghost_send,
    ghost_recv,
    slot_send,
    slot_recv,
    mark_send,
    mark_recv,
    part_send,
    part_recv,
):
    height, entries, tile = 2 * a_low.shape[0], a_low.shape[1], a_low.shape[2]
    capacity = ghost_out.shape[1]
    coarse = CB * rows
    column_count = out_ref.shape[1]
    per_part = height // PARTS
    zero_block = height + 2 * capacity
    pairs = (entries + SPAN) // 2
    s = lax.axis_index("row")
    k = lax.axis_index("col")
    after, before = lax.rem(s + 1, rows), lax.rem(s + rows - 1, rows)
    mate = k + 1 - 2 * lax.rem(k, 2)
    across = lax.rem(k + 2, 4)
    odd = lax.rem(k, 2)
    late = 1 - lax.rem(k // 2 + s, 2)

    barrier = pltpu.get_barrier_semaphore()
    for device in ({"row": before}, {"row": after}, {"col": mate}, {"col": across}):
        pl.semaphore_signal(barrier, inc=1, device_id=device, device_id_type=MESH)

    small = [
        pltpu.make_async_copy(source, target, small_sem.at[n])
        for n, (source, target) in enumerate(
            (
                (p_hbm, p_ref),
                (send_rows_ref, send_rows),
                (p_cols_ref, p_cols),
                (a_cols_ref, a_cols),
            )
        )
    ]
    for copy in small:
        copy.start()

    half = height // 2

    def a_copy(target, first, i):
        return pltpu.make_async_copy(a_ref.at[first + i], target.at[i], a_sem.at[first + i])

    def start_a(target, first):
        def one(i, carry):
            a_copy(target, first, i).start()
            return carry

        lax.fori_loop(0, half, one, 0)

    def wait_a(target, first):
        def one(i, carry):
            a_copy(target, first, i).wait()
            return carry

        lax.fori_loop(0, half, one, 0)

    start_a(a_low, 0)

    def first_id(slab):
        return lax.rem(CB * slab + coarse - 4, coarse)

    def first_column(slab):
        start = first_id(slab)
        offset = lax.rem(k + 4 - lax.rem(start, 4), 4)
        return lax.rem((start + offset) // 4, column_count)

    def place_group(place):
        return jnp.where(place >= 4, 1, 0) + jnp.where(place >= 8, 1, 0)

    start = first_id(s)
    left_start = lax.rem(CB * s + coarse - 2, coarse)
    for copy in small:
        copy.wait()

    for side in range(2):
        for t in range(capacity):
            row = send_rows[side, t]
            ghost_out[side, t] = p_ref[row, 0]
            ghost_out_ids[side, t : t + 1] = jnp.full((1, tile), p_cols[row], jnp.int32)
    padded[...] = jnp.zeros_like(padded)
    padded[:, :entries] = a_cols[...]
    listed = padded[...]

    pl.semaphore_wait(barrier, 4)

    def ghost_copies(side):
        target = {"row": after if side == 0 else before}
        return [
            pltpu.make_async_remote_copy(
                src_ref=src.at[side],
                dst_ref=dst.at[side],
                send_sem=ghost_send.at[side, n],
                recv_sem=ghost_recv.at[side, n],
                device_id=target,
                device_id_type=MESH,
            )
            for n, (src, dst) in enumerate(((ghost_out, ghost_in), (ghost_out_ids, ghost_in_ids)))
        ]

    hops = {1: (0, mate), 2: (0, across), 3: (2, mate)}

    def slot_copy(hop, part):
        source, target = hops[hop]
        return pltpu.make_async_remote_copy(
            src_ref=slots.at[source, part],
            dst_ref=slots.at[hop, part],
            send_sem=slot_send.at[hop - 1, part],
            recv_sem=slot_recv.at[hop - 1, part],
            device_id={"col": target},
            device_id_type=MESH,
        )

    def mark_copy(hop):
        source, target = hops[hop]
        return pltpu.make_async_remote_copy(
            src_ref=marks.at[source],
            dst_ref=marks.at[hop],
            send_sem=mark_send.at[hop - 1],
            recv_sem=mark_recv.at[hop - 1],
            device_id={"col": target},
            device_id_type=MESH,
        )

    def send_slot(hop):
        mark_copy(hop).start()
        for part in range(PARTS):
            slot_copy(hop, part).start()

    def receive_slot(hop):
        mark_copy(hop).wait_recv()
        for part in range(PARTS):
            slot_copy(hop, part).wait_recv()

    def forward(part):
        slot_copy(2, part).wait_recv()
        slot_copy(3, part).start()

    def forward_mark():
        mark_copy(2).wait_recv()
        mark_copy(3).start()

    for side in range(2):
        for copy in ghost_copies(side):
            copy.start()

    def own_part(part, group):
        for n in range(per_part):
            i = part * per_part + n
            block = p_ref[i, 0]
            blocks[i] = block
            slots[0, part, :, n * tile : (n + 1) * tile] = block.T
            place = wrap(p_cols[i] - left_start, coarse)
            marks[0, pl.ds(i, 1)] = jnp.full((1, tile), jnp.where(place >= 4, 1.0, 0.0), jnp.float32)
            group = group + jnp.where(listed == i, place_group(wrap(p_cols[i] - start, coarse)), 0)

        @pl.when(odd == 0)
        def _():
            slot_copy(2, part).start()

        slot_copy(1, part).start()
        return group

    group = lax.fori_loop(0, PARTS, own_part, jnp.zeros_like(listed))

    mark_copy(1).start()

    @pl.when(odd == 0)
    def _():
        mark_copy(2).start()

    start_a(a_high, half)

    blocks[zero_block] = jnp.zeros((tile, tile), jnp.bfloat16)
    for running in (running_even, running_odd):
        running[pairs] = jnp.zeros((tile, tile), jnp.float32)

    def clear(c, carry):
        for r in range(CB):
            out_ref[r, c] = jnp.zeros((tile, tile), jnp.float32)
        return carry

    lax.fori_loop(0, column_count, clear, 0)

    for side in range(2):
        for copy in ghost_copies(side):
            copy.wait_recv()
        for t in range(capacity):
            j = height + side * capacity + t
            blocks[j] = ghost_in[side, t]
            place = wrap(ghost_in_ids[side, t : t + 1] - start, coarse)
            group = group + jnp.where(listed == j, place_group(place), 0)

    @pl.when(odd == 1)
    def _():
        send_slot(2)

    lane = lax.broadcasted_iota(jnp.int32, listed.shape, 1)
    byte = jnp.where(group == 0, 1, jnp.where(group == 1, 1 << 8, 1 << 16))
    scan = jnp.where(lane < entries, byte, 0)
    step = 1
    while step < entries:
        scan = scan + jnp.where(lane >= step, pltpu.roll(scan, step, 1), 0)
        step *= 2
    total_counts = scan[:, entries - 1 : entries]
    counts = [(total_counts >> (8 * g)) & 255 for g in range(SPAN)]
    sizes = [((c + 1) >> 1) << 1 for c in counts]
    starts = [jnp.zeros_like(sizes[0]), sizes[0], sizes[0] + sizes[1]]
    slot = jnp.zeros_like(listed)
    for g in range(SPAN):
        slot = slot + jnp.where(group == g, starts[g] + ((scan >> (8 * g)) & 255) - 1, 0)
    packed = jnp.zeros_like(listed)
    for m in range(entries):
        packed = packed + jnp.where(
            slot[:, m : m + 1] == lane, (listed[:, m : m + 1] - zero_block) * 32 + m, 0
        )
    chosen = packed & 31
    column = (packed >> 5) + zero_block
    facts = jnp.ones_like(listed)
    for g in range(SPAN):
        facts = jnp.where(2 * lane == starts[g], 0, facts)
    for g in range(SPAN):
        last = jnp.where(counts[g] > 0, ((starts[g] + sizes[g]) >> 1) - 1, pairs)
        facts = jnp.where(lane == 16 + g, last, facts)
    table_v[...] = jnp.where(
        lane < 32,
        chosen,
        jnp.where(lane < 64, pltpu.roll(column, 32, 1), pltpu.roll(facts, 64, 1)),
    )
    table_copy = pltpu.make_async_copy(table_v, table, table_sem)
    table_copy.start()
    table_copy.wait()
    wait_a(a_low, 0)

    def group_row(source, first, n_row, running):
        i = first + n_row
        total = None
        for pair in range(pairs):
            at = (2 * pair, 2 * pair + 1)
            left = jnp.concatenate([source[n_row, table[i, n]] for n in at], axis=1)
            right = jnp.concatenate([blocks[table[i, 32 + n]] for n in at], axis=0)
            term = jnp.dot(left, right, preferred_element_type=jnp.float32)
            total = term if pair == 0 else jnp.where(table[i, 64 + pair] > 0, total, 0.0) + term
            running[pair] = total
        rows_of = pl.ds(pl.multiple_of(i * tile, tile), tile)
        for g in range(SPAN):
            grouped[rows_of, g * tile : (g + 1) * tile] = running[table[i, 80 + g]].astype(jnp.bfloat16)

    def multiply(source, first):
        def two(both, carry):
            group_row(source, first, 2 * both, running_even)
            group_row(source, first, 2 * both + 1, running_odd)

            @pl.when((odd == 0) & (first + 2 * both == height * 3 // 4))
            def _():
                forward(2)
                forward(3)

            return carry

        lax.fori_loop(0, half // 2, two, 0)

    multiply(a_low, 0)

    @pl.when(odd == 0)
    def _():
        forward_mark()
        forward(0)
        forward(1)

    wait_a(a_high, half)
    multiply(a_high, half)

    own_column = first_column(s)

    def part_copy(side, o, wide):
        columns = pl.ds(SPAN - 1, 1) if wide else pl.ds(0, SPAN - 1)
        return pltpu.make_async_remote_copy(
            src_ref=part_out.at[side, o, columns],
            dst_ref=part_in.at[side, o, columns],
            send_sem=part_send.at[side, o, wide],
            recv_sem=part_recv.at[side, o, wide],
            device_id={"row": before if side == 0 else after},
            device_id_type=MESH,
        )

    @pl.when(odd == 1)
    def _():
        forward_mark()
        for part in range(PARTS - 1):
            forward(part)

    receive_slot(1)

    def use_slot(step, carry):
        second = lax.rem(step, 2)
        others = step == 2 * (1 - late) + second

        @pl.when(others & (odd + second == 1))
        def _():
            receive_slot(3)

        @pl.when(others & (odd == 1) & (second == 1))
        def _():
            forward(PARTS - 1)

        index = lax.rem(2 * late + 2 * (step // 2), 4) + odd + second - 2 * odd * second
        total = None
        for part in range(PARTS):
            left = slots[index, part]
            mark = jnp.concatenate(
                [marks[index, part * per_part + n : part * per_part + n + 1] for n in range(per_part)],
                axis=1,
            )
            high = (left.astype(jnp.float32) * mark).astype(jnp.bfloat16)
            left = jnp.concatenate([left - high, high], axis=0)
            depth = per_part * tile
            term = jnp.dot(
                left, grouped[part * depth : (part + 1) * depth], preferred_element_type=jnp.float32
            )
            total = term if total is None else total + term

        @pl.when(step < 2)
        def _():
            for g in range(SPAN):
                columns = slice(g * tile, (g + 1) * tile)
                part_out[0, second, g] = total[:tile, columns].astype(jnp.bfloat16)
                part_out[1, second, g] = total[tile:, columns].astype(jnp.bfloat16)
            for side in range(2):
                part_copy(side, second, 0).start()

            @pl.when(late == 1)
            def _():
                for side in range(2):
                    part_copy(side, second, 1).start()

        @pl.when(step >= 2)
        def _():
            for g in range(SPAN):
                out_ref[second, lax.rem(own_column + g, column_count)] = total[
                    :tile, g * tile : (g + 1) * tile
                ]

        return carry

    lax.fori_loop(0, 4, use_slot, 0)

    columns_in = [first_column(after), first_column(before)]

    def collect(o, carry):
        for side in range(2):

            def add(g):
                at = lax.rem(columns_in[side] + g, column_count)
                out_ref[o, at] = out_ref[o, at] + part_in[side, o, g].astype(jnp.float32)

            part_copy(side, o, 0).wait_recv()
            for g in range(SPAN - 1):
                add(g)

            @pl.when(late == 0)
            def _():
                part_copy(side, o, 1).wait_recv()
                add(SPAN - 1)

        return carry

    lax.fori_loop(0, CB, collect, 0)

    for side in range(2):
        for copy in ghost_copies(side):
            copy.wait_send()
        for o in range(CB):
            part_copy(side, o, 0).wait_send()

    @pl.when(late == 1)
    def _():
        for side in range(2):
            for o in range(CB):
                part_copy(side, o, 1).wait_send()

    for hop in (1, 2, 3):
        mark_copy(hop).wait_send()
        for part in range(PARTS):
            slot_copy(hop, part).wait_send()


def shards(a_tiles, a_cols, p_tiles, p_cols, send_rows):
    rows, cols = lax.axis_size("row"), lax.axis_size("col")
    assert cols == 4
    height, entries, tile, _ = a_tiles.shape
    capacity = send_rows.shape[1]
    column_count = CB * rows // cols
    width = SPAN * tile
    vmem = pl.BlockSpec(memory_space=pltpu.VMEM)
    operands = (a_cols, p_cols.reshape(height), send_rows, p_tiles, a_tiles)
    bf16, f32, i32 = jnp.bfloat16, jnp.float32, jnp.int32
    dma = pltpu.SemaphoreType.DMA
    return pl.pallas_call(
        functools.partial(kernel, rows),
        out_shape=jax.ShapeDtypeStruct((CB, column_count, tile, tile), f32),
        in_specs=[pl.BlockSpec(memory_space=pltpu.HBM)] * 5,
        out_specs=vmem,
        scratch_shapes=[
            pltpu.VMEM(a_cols.shape, i32),
            pltpu.SMEM((height,), i32),
            pltpu.SMEM(send_rows.shape, i32),
            pltpu.VMEM(p_tiles.shape, bf16),
            pltpu.VMEM((height // 2,) + a_tiles.shape[1:], bf16),
            pltpu.VMEM((height // 2,) + a_tiles.shape[1:], bf16),
            pltpu.VMEM((2, capacity, tile, tile), bf16),
            pltpu.VMEM((2, 8, tile), i32),
            pltpu.VMEM((2, capacity, tile, tile), bf16),
            pltpu.VMEM((2, 8, tile), i32),
            pltpu.VMEM((4, PARTS, tile, height // PARTS * tile), bf16),
            pltpu.VMEM((4, height, tile), f32),
            pltpu.VMEM((height + 2 * capacity + 1, tile, tile), bf16),
            pltpu.VMEM(((entries + SPAN) // 2 + 1, tile, tile), f32),
            pltpu.VMEM(((entries + SPAN) // 2 + 1, tile, tile), f32),
            pltpu.VMEM((height, 128), i32),
            pltpu.VMEM((height, 128), i32),
            pltpu.SMEM((height, 128), i32),
            pltpu.VMEM((height * tile, width), bf16),
            pltpu.VMEM((2, CB, SPAN, tile, tile), bf16),
            pltpu.VMEM((2, CB, SPAN, tile, tile), bf16),
            dma((4,)),
            dma,
            dma((height,)),
            dma((2, 2)),
            dma((2, 2)),
            dma((3, PARTS)),
            dma((3, PARTS)),
            dma((3,)),
            dma((3,)),
            dma((2, CB, 2)),
            dma((2, CB, 2)),
        ],
        compiler_params=pltpu.CompilerParams(
            collective_id=0, has_side_effects=True, vmem_limit_bytes=48 * 1024 * 1024
        ),
        cost_estimate=pl.CostEstimate(
            flops=2 * height * entries * tile * tile * width,
            bytes_accessed=2 * a_tiles.size,
            transcendentals=0,
        ),
    )(*(pltpu.with_memory_space_constraint(x, pltpu.HBM) for x in operands))


def solution(mesh):
    in_specs = (
        P("row", None, None, None),
        P("row", None),
        P("row", "col", None, None),
        P("row", "col"),
        P("row", None),
    )
    out_specs = P("row", "col", None, None)
    return jax.shard_map(shards, mesh=mesh, in_specs=in_specs, out_specs=out_specs, check_vma=False)
```

```python
import functools

import jax
import jax.numpy as jnp
from jax import lax
from jax.experimental import pallas as pl
from jax.experimental.pallas import tpu as pltpu
from jax.sharding import PartitionSpec as P

CB = 2
SPAN = 3
PARTS = 4
MESH = pl.DeviceIdType.MESH


def wrap(value, size):
    return jnp.where(value < 0, value + size, value)


def kernel(
    rows,
    a_cols_ref,
    p_cols_ref,
    send_rows_ref,
    p_hbm,
    a_ref,
    out_ref,
    a_cols,
    p_cols,
    send_rows,
    p_ref,
    a_buf,
    ghost_out,
    ghost_out_ids,
    ghost_in,
    ghost_in_ids,
    slots,
    marks,
    blocks,
    running_even,
    running_odd,
    padded,
    table_v,
    table,
    grouped,
    part_out,
    part_in,
    small_sem,
    table_sem,
    a_sem,
    ghost_send,
    ghost_recv,
    slot_send,
    slot_recv,
    mark_send,
    mark_recv,
    part_send,
    part_recv,
):
    height, entries, tile = a_buf.shape[0], a_buf.shape[1], a_buf.shape[2]
    capacity = ghost_out.shape[1]
    coarse = CB * rows
    column_count = out_ref.shape[1]
    per_part = height // PARTS
    zero_block = height + 2 * capacity
    pairs = (entries + SPAN) // 2
    s = lax.axis_index("row")
    k = lax.axis_index("col")
    after, before = lax.rem(s + 1, rows), lax.rem(s + rows - 1, rows)
    mate = k + 1 - 2 * lax.rem(k, 2)
    across = lax.rem(k + 2, 4)
    odd = lax.rem(k, 2)
    late = 1 - lax.rem(k // 2 + s, 2)

    barrier = pltpu.get_barrier_semaphore()
    for device in ({"row": before}, {"row": after}, {"col": mate}, {"col": across}):
        pl.semaphore_signal(barrier, inc=1, device_id=device, device_id_type=MESH)

    small = [
        pltpu.make_async_copy(source, target, small_sem.at[n])
        for n, (source, target) in enumerate(
            (
                (p_hbm, p_ref),
                (send_rows_ref, send_rows),
                (p_cols_ref, p_cols),
                (a_cols_ref, a_cols),
            )
        )
    ]
    for copy in small:
        copy.start()

    def a_copy(i):
        return pltpu.make_async_copy(a_ref.at[i], a_buf.at[i], a_sem.at[i])

    def start_a(i, carry):
        a_copy(i).start()
        return carry

    def wait_a(i, carry):
        a_copy(i).wait()
        return carry

    lax.fori_loop(0, height // 2, start_a, 0)

    def first_id(slab):
        return lax.rem(CB * slab + coarse - 4, coarse)

    def first_column(slab):
        start = first_id(slab)
        offset = lax.rem(k + 4 - lax.rem(start, 4), 4)
        return lax.rem((start + offset) // 4, column_count)

    def place_group(place):
        return jnp.where(place >= 4, 1, 0) + jnp.where(place >= 8, 1, 0)

    start = first_id(s)
    left_start = lax.rem(CB * s + coarse - 2, coarse)
    for copy in small:
        copy.wait()

    for side in range(2):
        for t in range(capacity):
            row = send_rows[side, t]
            ghost_out[side, t] = p_ref[row, 0]
            ghost_out_ids[side, t : t + 1] = jnp.full((1, tile), p_cols[row], jnp.int32)
    padded[...] = jnp.zeros_like(padded)
    padded[:, :entries] = a_cols[...]
    listed = padded[...]

    pl.semaphore_wait(barrier, 4)

    def ghost_copies(side):
        target = {"row": after if side == 0 else before}
        return [
            pltpu.make_async_remote_copy(
                src_ref=src.at[side],
                dst_ref=dst.at[side],
                send_sem=ghost_send.at[side, n],
                recv_sem=ghost_recv.at[side, n],
                device_id=target,
                device_id_type=MESH,
            )
            for n, (src, dst) in enumerate(((ghost_out, ghost_in), (ghost_out_ids, ghost_in_ids)))
        ]

    hops = {1: (0, mate), 2: (0, across), 3: (2, mate)}

    def slot_copy(hop, part):
        source, target = hops[hop]
        return pltpu.make_async_remote_copy(
            src_ref=slots.at[source, part],
            dst_ref=slots.at[hop, part],
            send_sem=slot_send.at[hop - 1, part],
            recv_sem=slot_recv.at[hop - 1, part],
            device_id={"col": target},
            device_id_type=MESH,
        )

    def mark_copy(hop):
        source, target = hops[hop]
        return pltpu.make_async_remote_copy(
            src_ref=marks.at[source],
            dst_ref=marks.at[hop],
            send_sem=mark_send.at[hop - 1],
            recv_sem=mark_recv.at[hop - 1],
            device_id={"col": target},
            device_id_type=MESH,
        )

    def receive_slot(hop):
        mark_copy(hop).wait_recv()
        for part in range(PARTS):
            slot_copy(hop, part).wait_recv()

    def forward(part):
        slot_copy(2, part).wait_recv()
        slot_copy(3, part).start()

    def forward_mark():
        mark_copy(2).wait_recv()
        mark_copy(3).start()

    for side in range(2):
        for copy in ghost_copies(side):
            copy.start()

    def own_part(part, group):
        for n in range(per_part):
            i = part * per_part + n
            block = p_ref[i, 0]
            blocks[i] = block
            slots[0, part, :, n * tile : (n + 1) * tile] = block.T
            place = wrap(p_cols[i] - left_start, coarse)
            marks[0, pl.ds(i, 1)] = jnp.full((1, tile), jnp.where(place >= 4, 1.0, 0.0), jnp.float32)
            group = group + jnp.where(listed == i, place_group(wrap(p_cols[i] - start, coarse)), 0)

        for hop in (2, 1):
            slot_copy(hop, part).start()
        return group

    group = lax.fori_loop(0, PARTS, own_part, jnp.zeros_like(listed))

    for hop in (2, 1):
        mark_copy(hop).start()
    lax.fori_loop(height // 2, height, start_a, 0)

    blocks[zero_block] = jnp.zeros((tile, tile), jnp.bfloat16)
    for running in (running_even, running_odd):
        running[pairs] = jnp.zeros((tile, tile), jnp.float32)

    def clear(c, carry):
        for r in range(CB):
            out_ref[r, c] = jnp.zeros((tile, tile), jnp.float32)
        return carry

    lax.fori_loop(0, column_count, clear, 0)

    for side in range(2):
        for copy in ghost_copies(side):
            copy.wait_recv()
        for t in range(capacity):
            j = height + side * capacity + t
            blocks[j] = ghost_in[side, t]
            place = wrap(ghost_in_ids[side, t : t + 1] - start, coarse)
            group = group + jnp.where(listed == j, place_group(place), 0)

    lane = lax.broadcasted_iota(jnp.int32, listed.shape, 1)
    byte = jnp.where(group == 0, 1, jnp.where(group == 1, 1 << 8, 1 << 16))
    scan = jnp.where(lane < entries, byte, 0)
    step = 1
    while step < entries:
        scan = scan + jnp.where(lane >= step, pltpu.roll(scan, step, 1), 0)
        step *= 2
    total_counts = scan[:, entries - 1 : entries]
    counts = [(total_counts >> (8 * g)) & 255 for g in range(SPAN)]
    sizes = [((c + 1) >> 1) << 1 for c in counts]
    starts = [jnp.zeros_like(sizes[0]), sizes[0], sizes[0] + sizes[1]]
    slot = jnp.zeros_like(listed)
    for g in range(SPAN):
        slot = slot + jnp.where(group == g, starts[g] + ((scan >> (8 * g)) & 255) - 1, 0)
    packed = jnp.zeros_like(listed)
    for m in range(entries):
        packed = packed + jnp.where(
            slot[:, m : m + 1] == lane, (listed[:, m : m + 1] - zero_block) * 32 + m, 0
        )
    chosen = packed & 31
    column = (packed >> 5) + zero_block
    facts = jnp.ones_like(listed)
    for g in range(SPAN):
        facts = jnp.where(2 * lane == starts[g], 0, facts)
    for g in range(SPAN):
        last = jnp.where(counts[g] > 0, ((starts[g] + sizes[g]) >> 1) - 1, pairs)
        facts = jnp.where(lane == 16 + g, last, facts)
    table_v[...] = jnp.where(
        lane < 32,
        chosen,
        jnp.where(lane < 64, pltpu.roll(column, 32, 1), pltpu.roll(facts, 64, 1)),
    )
    table_copy = pltpu.make_async_copy(table_v, table, table_sem)
    table_copy.start()
    table_copy.wait()
    lax.fori_loop(0, height, wait_a, 0)

    def group_row(i, running):
        total = None
        for pair in range(pairs):
            at = (2 * pair, 2 * pair + 1)
            left = jnp.concatenate([a_buf[i, table[i, n]] for n in at], axis=1)
            right = jnp.concatenate([blocks[table[i, 32 + n]] for n in at], axis=0)
            term = jnp.dot(left, right, preferred_element_type=jnp.float32)
            total = term if pair == 0 else jnp.where(table[i, 64 + pair] > 0, total, 0.0) + term
            running[pair] = total
        rows_of = pl.ds(pl.multiple_of(i * tile, tile), tile)
        for g in range(SPAN):
            grouped[rows_of, g * tile : (g + 1) * tile] = running[table[i, 80 + g]].astype(jnp.bfloat16)

    def multiply(both, carry):
        i = 2 * both
        group_row(i, running_even)
        group_row(i + 1, running_odd)

        @pl.when(i == height // 2)
        def _():
            forward_mark()
            forward(0)
            forward(1)

        @pl.when(i == height * 3 // 4)
        def _():
            forward(2)

        return carry

    lax.fori_loop(0, height // 2, multiply, 0)

    own_column = first_column(s)

    def part_copy(side, o, wide):
        columns = pl.ds(SPAN - 1, 1) if wide else pl.ds(0, SPAN - 1)
        return pltpu.make_async_remote_copy(
            src_ref=part_out.at[side, o, columns],
            dst_ref=part_in.at[side, o, columns],
            send_sem=part_send.at[side, o, wide],
            recv_sem=part_recv.at[side, o, wide],
            device_id={"row": before if side == 0 else after},
            device_id_type=MESH,
        )

    forward(PARTS - 1)
    receive_slot(1)

    def use_slot(step, carry):
        from_mate = lax.rem(step, 2)
        second = odd + from_mate - 2 * odd * from_mate

        @pl.when(step == 2 * (1 - late) + 1)
        def _():
            receive_slot(3)

        index = lax.rem(2 * late + 2 * (step // 2), 4) + from_mate
        total = None
        for part in range(PARTS):
            left = slots[index, part]
            mark = jnp.concatenate(
                [marks[index, part * per_part + n : part * per_part + n + 1] for n in range(per_part)],
                axis=1,
            )
            high = (left.astype(jnp.float32) * mark).astype(jnp.bfloat16)
            left = jnp.concatenate([left - high, high], axis=0)
            depth = per_part * tile
            term = jnp.dot(
                left, grouped[part * depth : (part + 1) * depth], preferred_element_type=jnp.float32
            )
            total = term if total is None else total + term

        @pl.when(step < 2)
        def _():
            for g in range(SPAN):
                columns = slice(g * tile, (g + 1) * tile)
                part_out[0, second, g] = total[:tile, columns].astype(jnp.bfloat16)
                part_out[1, second, g] = total[tile:, columns].astype(jnp.bfloat16)
            for side in range(2):
                part_copy(side, second, 0).start()

            @pl.when(late == 1)
            def _():
                for side in range(2):
                    part_copy(side, second, 1).start()

        @pl.when(step >= 2)
        def _():
            for g in range(SPAN):
                out_ref[second, lax.rem(own_column + g, column_count)] = total[
                    :tile, g * tile : (g + 1) * tile
                ]

        return carry

    lax.fori_loop(0, 4, use_slot, 0)

    columns_in = [first_column(after), first_column(before)]

    def collect(o, carry):
        for side in range(2):

            def add(g):
                at = lax.rem(columns_in[side] + g, column_count)
                out_ref[o, at] = out_ref[o, at] + part_in[side, o, g].astype(jnp.float32)

            part_copy(side, o, 0).wait_recv()
            for g in range(SPAN - 1):
                add(g)

            @pl.when(late == 0)
            def _():
                part_copy(side, o, 1).wait_recv()
                add(SPAN - 1)

        return carry

    lax.fori_loop(0, CB, collect, 0)

    for side in range(2):
        for copy in ghost_copies(side):
            copy.wait_send()
        for o in range(CB):
            part_copy(side, o, 0).wait_send()

    @pl.when(late == 1)
    def _():
        for side in range(2):
            for o in range(CB):
                part_copy(side, o, 1).wait_send()

    for hop in (1, 2, 3):
        mark_copy(hop).wait_send()
        for part in range(PARTS):
            slot_copy(hop, part).wait_send()


def shards(a_tiles, a_cols, p_tiles, p_cols, send_rows):
    rows, cols = lax.axis_size("row"), lax.axis_size("col")
    assert cols == 4
    height, entries, tile, _ = a_tiles.shape
    capacity = send_rows.shape[1]
    column_count = CB * rows // cols
    width = SPAN * tile
    vmem = pl.BlockSpec(memory_space=pltpu.VMEM)
    operands = (a_cols, p_cols.reshape(height), send_rows, p_tiles, a_tiles)
    bf16, f32, i32 = jnp.bfloat16, jnp.float32, jnp.int32
    dma = pltpu.SemaphoreType.DMA
    return pl.pallas_call(
        functools.partial(kernel, rows),
        out_shape=jax.ShapeDtypeStruct((CB, column_count, tile, tile), f32),
        in_specs=[pl.BlockSpec(memory_space=pltpu.HBM)] * 5,
        out_specs=vmem,
        scratch_shapes=[
            pltpu.VMEM(a_cols.shape, i32),
            pltpu.SMEM((height,), i32),
            pltpu.SMEM(send_rows.shape, i32),
            pltpu.VMEM(p_tiles.shape, bf16),
            pltpu.VMEM(a_tiles.shape, bf16),
            pltpu.VMEM((2, capacity, tile, tile), bf16),
            pltpu.VMEM((2, 8, tile), i32),
            pltpu.VMEM((2, capacity, tile, tile), bf16),
            pltpu.VMEM((2, 8, tile), i32),
            pltpu.VMEM((4, PARTS, tile, height // PARTS * tile), bf16),
            pltpu.VMEM((4, height, tile), f32),
            pltpu.VMEM((height + 2 * capacity + 1, tile, tile), bf16),
            pltpu.VMEM(((entries + SPAN) // 2 + 1, tile, tile), f32),
            pltpu.VMEM(((entries + SPAN) // 2 + 1, tile, tile), f32),
            pltpu.VMEM((height, 128), i32),
            pltpu.VMEM((height, 128), i32),
            pltpu.SMEM((height, 128), i32),
            pltpu.VMEM((height * tile, width), bf16),
            pltpu.VMEM((2, CB, SPAN, tile, tile), bf16),
            pltpu.VMEM((2, CB, SPAN, tile, tile), bf16),
            dma((4,)),
            dma,
            dma((height,)),
            dma((2, 2)),
            dma((2, 2)),
            dma((3, PARTS)),
            dma((3, PARTS)),
            dma((3,)),
            dma((3,)),
            dma((2, CB, 2)),
            dma((2, CB, 2)),
        ],
        compiler_params=pltpu.CompilerParams(
            collective_id=0, has_side_effects=True, vmem_limit_bytes=48 * 1024 * 1024
        ),
        cost_estimate=pl.CostEstimate(
            flops=2 * height * entries * tile * tile * width,
            bytes_accessed=2 * a_tiles.size,
            transcendentals=0,
        ),
    )(*(pltpu.with_memory_space_constraint(x, pltpu.HBM) for x in operands))


def solution(mesh):
    in_specs = (
        P("row", None, None, None),
        P("row", None),
        P("row", "col", None, None),
        P("row", "col"),
        P("row", None),
    )
    out_specs = P("row", "col", None, None)
    return jax.shard_map(shards, mesh=mesh, in_specs=in_specs, out_specs=out_specs, check_vma=False)
```

```python
import functools

import jax
import jax.numpy as jnp
from jax import lax
from jax.experimental import pallas as pl
from jax.experimental.pallas import tpu as pltpu
from jax.sharding import PartitionSpec as P

CB = 2
SPAN = 3
PARTS = 4
MESH = pl.DeviceIdType.MESH


def wrap(value, size):
    return jnp.where(value < 0, value + size, value)


def kernel(
    rows,
    a_cols_ref,
    p_cols_ref,
    send_rows_ref,
    p_hbm,
    a_ref,
    out_ref,
    a_cols,
    p_cols,
    send_rows,
    p_ref,
    a_buf,
    ghost_out,
    ghost_out_ids,
    ghost_in,
    ghost_in_ids,
    slots,
    marks,
    blocks,
    running_even,
    running_odd,
    padded,
    table_v,
    table,
    grouped,
    part_out,
    part_in,
    small_sem,
    table_sem,
    a_sem,
    ghost_send,
    ghost_recv,
    slot_send,
    slot_recv,
    mark_send,
    mark_recv,
    part_send,
    part_recv,
):
    height, entries, tile = a_buf.shape[0], a_buf.shape[1], a_buf.shape[2]
    capacity = ghost_out.shape[1]
    coarse = CB * rows
    column_count = out_ref.shape[1]
    per_part = height // PARTS
    zero_block = height + 2 * capacity
    pairs = (entries + SPAN) // 2
    s = lax.axis_index("row")
    k = lax.axis_index("col")
    after, before = lax.rem(s + 1, rows), lax.rem(s + rows - 1, rows)
    mate = k + 1 - 2 * lax.rem(k, 2)
    across = lax.rem(k + 2, 4)
    odd = lax.rem(k, 2)
    late = 1 - lax.rem(k // 2 + s, 2)

    barrier = pltpu.get_barrier_semaphore()
    for device in ({"row": before}, {"row": after}, {"col": mate}, {"col": across}):
        pl.semaphore_signal(barrier, inc=1, device_id=device, device_id_type=MESH)

    small = [
        pltpu.make_async_copy(source, target, small_sem.at[n])
        for n, (source, target) in enumerate(
            (
                (p_hbm, p_ref),
                (send_rows_ref, send_rows),
                (p_cols_ref, p_cols),
                (a_cols_ref, a_cols),
            )
        )
    ]
    for copy in small:
        copy.start()

    def a_copy(i):
        return pltpu.make_async_copy(a_ref.at[i], a_buf.at[i], a_sem.at[i])

    def start_a(i, carry):
        a_copy(i).start()
        return carry

    def wait_a(i, carry):
        a_copy(i).wait()
        return carry

    lax.fori_loop(0, height // 2, start_a, 0)

    def first_id(slab):
        return lax.rem(CB * slab + coarse - 4, coarse)

    def first_column(slab):
        start = first_id(slab)
        offset = lax.rem(k + 4 - lax.rem(start, 4), 4)
        return lax.rem((start + offset) // 4, column_count)

    def place_group(place):
        return jnp.where(place >= 4, 1, 0) + jnp.where(place >= 8, 1, 0)

    start = first_id(s)
    left_start = lax.rem(CB * s + coarse - 2, coarse)
    for copy in small:
        copy.wait()

    for side in range(2):
        for t in range(capacity):
            row = send_rows[side, t]
            ghost_out[side, t] = p_ref[row, 0]
            ghost_out_ids[side, t : t + 1] = jnp.full((1, tile), p_cols[row], jnp.int32)
    padded[...] = jnp.zeros_like(padded)
    padded[:, :entries] = a_cols[...]
    listed = padded[...]

    pl.semaphore_wait(barrier, 4)

    def ghost_copies(side):
        target = {"row": after if side == 0 else before}
        return [
            pltpu.make_async_remote_copy(
                src_ref=src.at[side],
                dst_ref=dst.at[side],
                send_sem=ghost_send.at[side, n],
                recv_sem=ghost_recv.at[side, n],
                device_id=target,
                device_id_type=MESH,
            )
            for n, (src, dst) in enumerate(((ghost_out, ghost_in), (ghost_out_ids, ghost_in_ids)))
        ]

    hops = {1: (0, mate), 2: (0, across), 3: (2, mate)}

    def slot_copy(hop, part):
        source, target = hops[hop]
        return pltpu.make_async_remote_copy(
            src_ref=slots.at[source, part],
            dst_ref=slots.at[hop, part],
            send_sem=slot_send.at[hop - 1, part],
            recv_sem=slot_recv.at[hop - 1, part],
            device_id={"col": target},
            device_id_type=MESH,
        )

    def mark_copy(hop):
        source, target = hops[hop]
        return pltpu.make_async_remote_copy(
            src_ref=marks.at[source],
            dst_ref=marks.at[hop],
            send_sem=mark_send.at[hop - 1],
            recv_sem=mark_recv.at[hop - 1],
            device_id={"col": target},
            device_id_type=MESH,
        )

    def send_slot(hop):
        mark_copy(hop).start()
        for part in range(PARTS):
            slot_copy(hop, part).start()

    def receive_slot(hop):
        mark_copy(hop).wait_recv()
        for part in range(PARTS):
            slot_copy(hop, part).wait_recv()

    def forward(part):
        slot_copy(2, part).wait_recv()
        slot_copy(3, part).start()

    def forward_mark():
        mark_copy(2).wait_recv()
        mark_copy(3).start()

    for side in range(2):
        for copy in ghost_copies(side):
            copy.start()

    def own_part(part, group):
        for n in range(per_part):
            i = part * per_part + n
            block = p_ref[i, 0]
            blocks[i] = block
            slots[0, part, :, n * tile : (n + 1) * tile] = block.T
            place = wrap(p_cols[i] - left_start, coarse)
            marks[0, pl.ds(i, 1)] = jnp.full((1, tile), jnp.where(place >= 4, 1.0, 0.0), jnp.float32)
            group = group + jnp.where(listed == i, place_group(wrap(p_cols[i] - start, coarse)), 0)

        @pl.when(odd == 0)
        def _():
            slot_copy(2, part).start()

        slot_copy(1, part).start()
        return group

    group = lax.fori_loop(0, PARTS, own_part, jnp.zeros_like(listed))

    mark_copy(1).start()

    @pl.when(odd == 0)
    def _():
        mark_copy(2).start()

    lax.fori_loop(height // 2, height, start_a, 0)

    blocks[zero_block] = jnp.zeros((tile, tile), jnp.bfloat16)
    for running in (running_even, running_odd):
        running[pairs] = jnp.zeros((tile, tile), jnp.float32)

    def clear(c, carry):
        for r in range(CB):
            out_ref[r, c] = jnp.zeros((tile, tile), jnp.float32)
        return carry

    lax.fori_loop(0, column_count, clear, 0)

    for side in range(2):
        for copy in ghost_copies(side):
            copy.wait_recv()
        for t in range(capacity):
            j = height + side * capacity + t
            blocks[j] = ghost_in[side, t]
            place = wrap(ghost_in_ids[side, t : t + 1] - start, coarse)
            group = group + jnp.where(listed == j, place_group(place), 0)

    @pl.when(odd == 1)
    def _():
        send_slot(2)

    lane = lax.broadcasted_iota(jnp.int32, listed.shape, 1)
    byte = jnp.where(group == 0, 1, jnp.where(group == 1, 1 << 8, 1 << 16))
    scan = jnp.where(lane < entries, byte, 0)
    step = 1
    while step < entries:
        scan = scan + jnp.where(lane >= step, pltpu.roll(scan, step, 1), 0)
        step *= 2
    total_counts = scan[:, entries - 1 : entries]
    counts = [(total_counts >> (8 * g)) & 255 for g in range(SPAN)]
    sizes = [((c + 1) >> 1) << 1 for c in counts]
    starts = [jnp.zeros_like(sizes[0]), sizes[0], sizes[0] + sizes[1]]
    slot = jnp.zeros_like(listed)
    for g in range(SPAN):
        slot = slot + jnp.where(group == g, starts[g] + ((scan >> (8 * g)) & 255) - 1, 0)
    packed = jnp.zeros_like(listed)
    for m in range(entries):
        packed = packed + jnp.where(
            slot[:, m : m + 1] == lane, (listed[:, m : m + 1] - zero_block) * 32 + m, 0
        )
    chosen = packed & 31
    column = (packed >> 5) + zero_block
    facts = jnp.ones_like(listed)
    for g in range(SPAN):
        facts = jnp.where(2 * lane == starts[g], 0, facts)
    for g in range(SPAN):
        last = jnp.where(counts[g] > 0, ((starts[g] + sizes[g]) >> 1) - 1, pairs)
        facts = jnp.where(lane == 16 + g, last, facts)
    table_v[...] = jnp.where(
        lane < 32,
        chosen,
        jnp.where(lane < 64, pltpu.roll(column, 32, 1), pltpu.roll(facts, 64, 1)),
    )
    table_copy = pltpu.make_async_copy(table_v, table, table_sem)
    table_copy.start()
    table_copy.wait()
    lax.fori_loop(0, height, wait_a, 0)

    def group_row(i, running):
        total = None
        for pair in range(pairs):
            at = (2 * pair, 2 * pair + 1)
            left = jnp.concatenate([a_buf[i, table[i, n]] for n in at], axis=1)
            right = jnp.concatenate([blocks[table[i, 32 + n]] for n in at], axis=0)
            term = jnp.dot(left, right, preferred_element_type=jnp.float32)
            total = term if pair == 0 else jnp.where(table[i, 64 + pair] > 0, total, 0.0) + term
            running[pair] = total
        rows_of = pl.ds(pl.multiple_of(i * tile, tile), tile)
        for g in range(SPAN):
            grouped[rows_of, g * tile : (g + 1) * tile] = running[table[i, 80 + g]].astype(jnp.bfloat16)

    def multiply(both, carry):
        i = 2 * both
        group_row(i, running_even)
        group_row(i + 1, running_odd)

        @pl.when((odd == 0) & (i == height // 2))
        def _():
            forward_mark()
            forward(0)
            forward(1)

        @pl.when((odd == 0) & (i == height * 3 // 4))
        def _():
            forward(2)
            forward(3)

        return carry

    lax.fori_loop(0, height // 2, multiply, 0)

    own_column = first_column(s)

    def part_copy(side, o, g):
        return pltpu.make_async_remote_copy(
            src_ref=part_out.at[side, o, g],
            dst_ref=part_in.at[side, o, g],
            send_sem=part_send.at[side, o, g],
            recv_sem=part_recv.at[side, o, g],
            device_id={"row": before if side == 0 else after},
            device_id_type=MESH,
        )

    @pl.when(odd == 1)
    def _():
        forward_mark()
        for part in range(PARTS - 1):
            forward(part)

    receive_slot(1)

    def use_slot(step, carry):
        second = lax.rem(step, 2)
        others = step == 2 * (1 - late) + second

        @pl.when(others & (odd + second == 1))
        def _():
            receive_slot(3)

        @pl.when(others & (odd == 1) & (second == 1))
        def _():
            forward(PARTS - 1)

        index = lax.rem(2 * late + 2 * (step // 2), 4) + odd + second - 2 * odd * second
        def one_column(g, inner):
            lanes = pl.ds(pl.multiple_of(g * tile, tile), tile)
            total = None
            for part in range(PARTS):
                left = slots[index, part]
                mark = jnp.concatenate(
                    [marks[index, part * per_part + n : part * per_part + n + 1] for n in range(per_part)],
                    axis=1,
                )
                high = left * mark.astype(jnp.bfloat16)
                left = jnp.concatenate([left - high, high], axis=0)
                depth = per_part * tile
                term = jnp.dot(
                    left,
                    grouped[part * depth : (part + 1) * depth, lanes],
                    preferred_element_type=jnp.float32,
                )
                total = term if total is None else total + term

            @pl.when(step < 2)
            def _():
                for side in range(2):
                    part_out[side, second, g] = total[side * tile : (side + 1) * tile].astype(jnp.bfloat16)
                    part_copy(side, second, g).start()

            @pl.when(step >= 2)
            def _():
                out_ref[second, lax.rem(own_column + g, column_count)] = total[:tile]

            return inner

        lax.fori_loop(0, SPAN - 1 + late, one_column, 0)
        return carry

    lax.fori_loop(0, 4, use_slot, 0)

    columns_in = [first_column(after), first_column(before)]

    def collect(o, carry):
        def add(g, inner):
            for side in range(2):
                part_copy(side, o, g).wait_recv()
                at = lax.rem(columns_in[side] + g, column_count)
                out_ref[o, at] = out_ref[o, at] + part_in[side, o, g].astype(jnp.float32)
            return inner

        lax.fori_loop(0, SPAN - late, add, 0)
        return carry

    lax.fori_loop(0, CB, collect, 0)

    for side in range(2):
        for copy in ghost_copies(side):
            copy.wait_send()

    def sent(g, carry):
        for side in range(2):
            for o in range(CB):
                part_copy(side, o, g).wait_send()
        return carry

    lax.fori_loop(0, SPAN - 1 + late, sent, 0)
    for hop in (1, 2, 3):
        mark_copy(hop).wait_send()
        for part in range(PARTS):
            slot_copy(hop, part).wait_send()


def shards(a_tiles, a_cols, p_tiles, p_cols, send_rows):
    rows, cols = lax.axis_size("row"), lax.axis_size("col")
    assert cols == 4
    height, entries, tile, _ = a_tiles.shape
    capacity = send_rows.shape[1]
    column_count = CB * rows // cols
    width = SPAN * tile
    vmem = pl.BlockSpec(memory_space=pltpu.VMEM)
    operands = (a_cols, p_cols.reshape(height), send_rows, p_tiles, a_tiles)
    bf16, f32, i32 = jnp.bfloat16, jnp.float32, jnp.int32
    dma = pltpu.SemaphoreType.DMA
    return pl.pallas_call(
        functools.partial(kernel, rows),
        out_shape=jax.ShapeDtypeStruct((CB, column_count, tile, tile), f32),
        in_specs=[pl.BlockSpec(memory_space=pltpu.HBM)] * 5,
        out_specs=vmem,
        scratch_shapes=[
            pltpu.VMEM(a_cols.shape, i32),
            pltpu.SMEM((height,), i32),
            pltpu.SMEM(send_rows.shape, i32),
            pltpu.VMEM(p_tiles.shape, bf16),
            pltpu.VMEM(a_tiles.shape, bf16),
            pltpu.VMEM((2, capacity, tile, tile), bf16),
            pltpu.VMEM((2, 8, tile), i32),
            pltpu.VMEM((2, capacity, tile, tile), bf16),
            pltpu.VMEM((2, 8, tile), i32),
            pltpu.VMEM((4, PARTS, tile, height // PARTS * tile), bf16),
            pltpu.VMEM((4, height, tile), f32),
            pltpu.VMEM((height + 2 * capacity + 1, tile, tile), bf16),
            pltpu.VMEM(((entries + SPAN) // 2 + 1, tile, tile), f32),
            pltpu.VMEM(((entries + SPAN) // 2 + 1, tile, tile), f32),
            pltpu.VMEM((height, 128), i32),
            pltpu.VMEM((height, 128), i32),
            pltpu.SMEM((height, 128), i32),
            pltpu.VMEM((height * tile, width), bf16),
            pltpu.VMEM((2, CB, SPAN, tile, tile), bf16),
            pltpu.VMEM((2, CB, SPAN, tile, tile), bf16),
            dma((4,)),
            dma,
            dma((height,)),
            dma((2, 2)),
            dma((2, 2)),
            dma((3, PARTS)),
            dma((3, PARTS)),
            dma((3,)),
            dma((3,)),
            dma((2, CB, SPAN)),
            dma((2, CB, SPAN)),
        ],
        compiler_params=pltpu.CompilerParams(
            collective_id=0, has_side_effects=True, vmem_limit_bytes=48 * 1024 * 1024
        ),
        cost_estimate=pl.CostEstimate(
            flops=2 * height * entries * tile * tile * width,
            bytes_accessed=2 * a_tiles.size,
            transcendentals=0,
        ),
    )(*(pltpu.with_memory_space_constraint(x, pltpu.HBM) for x in operands))


def solution(mesh):
    in_specs = (
        P("row", None, None, None),
        P("row", None),
        P("row", "col", None, None),
        P("row", "col"),
        P("row", None),
    )
    out_specs = P("row", "col", None, None)
    return jax.shard_map(shards, mesh=mesh, in_specs=in_specs, out_specs=out_specs, check_vma=False)
```

```python
import functools

import jax
import jax.numpy as jnp
from jax import lax
from jax.experimental import pallas as pl
from jax.experimental.pallas import tpu as pltpu
from jax.sharding import PartitionSpec as P

CB = 2
SPAN = 3
PARTS = 4
MESH = pl.DeviceIdType.MESH


def wrap(value, size):
    return jnp.where(value < 0, value + size, value)


def kernel(
    rows,
    a_cols_ref,
    p_cols_ref,
    send_rows_ref,
    p_hbm,
    a_ref,
    out_ref,
    a_cols,
    p_cols,
    send_rows,
    p_ref,
    a_buf,
    ghost_out,
    ghost_out_ids,
    ghost_in,
    ghost_in_ids,
    slots,
    marks,
    blocks,
    running_even,
    running_odd,
    padded,
    table_v,
    table,
    grouped,
    part_out,
    part_in,
    small_sem,
    table_sem,
    a_sem,
    ghost_send,
    ghost_recv,
    slot_send,
    slot_recv,
    mark_send,
    mark_recv,
    part_send,
    part_recv,
):
    height, entries, tile = a_buf.shape[0], a_buf.shape[1], a_buf.shape[2]
    capacity = ghost_out.shape[1]
    coarse = CB * rows
    column_count = out_ref.shape[1]
    per_part = height // PARTS
    zero_block = height + 2 * capacity
    pairs = (entries + SPAN) // 2
    s = lax.axis_index("row")
    k = lax.axis_index("col")
    after, before = lax.rem(s + 1, rows), lax.rem(s + rows - 1, rows)
    mate = k + 1 - 2 * lax.rem(k, 2)
    across = lax.rem(k + 2, 4)
    odd = lax.rem(k, 2)
    late = 1 - lax.rem(k // 2 + s, 2)

    barrier = pltpu.get_barrier_semaphore()
    for device in ({"row": before}, {"row": after}, {"col": mate}, {"col": across}):
        pl.semaphore_signal(barrier, inc=1, device_id=device, device_id_type=MESH)

    small = [
        pltpu.make_async_copy(source, target, small_sem.at[n])
        for n, (source, target) in enumerate(
            (
                (p_hbm, p_ref),
                (send_rows_ref, send_rows),
                (p_cols_ref, p_cols),
                (a_cols_ref, a_cols),
            )
        )
    ]
    for copy in small:
        copy.start()

    def a_copy(i):
        return pltpu.make_async_copy(a_ref.at[i], a_buf.at[i], a_sem.at[i])

    def start_a(i, carry):
        a_copy(i).start()
        return carry

    def wait_a(i, carry):
        a_copy(i).wait()
        return carry

    lax.fori_loop(0, height // 2, start_a, 0)

    def first_id(slab):
        return lax.rem(CB * slab + coarse - 4, coarse)

    def first_column(slab):
        start = first_id(slab)
        offset = lax.rem(k + 4 - lax.rem(start, 4), 4)
        return lax.rem((start + offset) // 4, column_count)

    def place_group(place):
        return jnp.where(place >= 4, 1, 0) + jnp.where(place >= 8, 1, 0)

    start = first_id(s)
    left_start = lax.rem(CB * s + coarse - 2, coarse)
    for copy in small:
        copy.wait()

    for side in range(2):
        for t in range(capacity):
            row = send_rows[side, t]
            ghost_out[side, t] = p_ref[row, 0]
            ghost_out_ids[side, t : t + 1] = jnp.full((1, tile), p_cols[row], jnp.int32)
    padded[...] = jnp.zeros_like(padded)
    padded[:, :entries] = a_cols[...]
    listed = padded[...]

    pl.semaphore_wait(barrier, 4)

    def ghost_copies(side):
        target = {"row": after if side == 0 else before}
        return [
            pltpu.make_async_remote_copy(
                src_ref=src.at[side],
                dst_ref=dst.at[side],
                send_sem=ghost_send.at[side, n],
                recv_sem=ghost_recv.at[side, n],
                device_id=target,
                device_id_type=MESH,
            )
            for n, (src, dst) in enumerate(((ghost_out, ghost_in), (ghost_out_ids, ghost_in_ids)))
        ]

    hops = {1: (0, mate), 2: (0, across), 3: (2, mate)}

    def slot_copy(hop, part):
        source, target = hops[hop]
        return pltpu.make_async_remote_copy(
            src_ref=slots.at[source, part],
            dst_ref=slots.at[hop, part],
            send_sem=slot_send.at[hop - 1, part],
            recv_sem=slot_recv.at[hop - 1, part],
            device_id={"col": target},
            device_id_type=MESH,
        )

    def mark_copy(hop):
        source, target = hops[hop]
        return pltpu.make_async_remote_copy(
            src_ref=marks.at[source],
            dst_ref=marks.at[hop],
            send_sem=mark_send.at[hop - 1],
            recv_sem=mark_recv.at[hop - 1],
            device_id={"col": target},
            device_id_type=MESH,
        )

    def send_slot(hop):
        mark_copy(hop).start()
        for part in range(PARTS):
            slot_copy(hop, part).start()

    def receive_slot(hop):
        mark_copy(hop).wait_recv()
        for part in range(PARTS):
            slot_copy(hop, part).wait_recv()

    def forward(part):
        slot_copy(2, part).wait_recv()
        slot_copy(3, part).start()

    def forward_mark():
        mark_copy(2).wait_recv()
        mark_copy(3).start()

    for side in range(2):
        for copy in ghost_copies(side):
            copy.start()

    def own_part(part, group):
        for n in range(per_part):
            i = part * per_part + n
            block = p_ref[i, 0]
            blocks[i] = block
            slots[0, part, :, n * tile : (n + 1) * tile] = block.T
            place = wrap(p_cols[i] - left_start, coarse)
            marks[0, pl.ds(i, 1)] = jnp.full((1, tile), jnp.where(place >= 4, 1.0, 0.0), jnp.float32)
            group = group + jnp.where(listed == i, place_group(wrap(p_cols[i] - start, coarse)), 0)

        @pl.when(odd == 0)
        def _():
            slot_copy(2, part).start()

        slot_copy(1, part).start()
        return group

    group = lax.fori_loop(0, PARTS, own_part, jnp.zeros_like(listed))

    mark_copy(1).start()

    @pl.when(odd == 0)
    def _():
        mark_copy(2).start()

    lax.fori_loop(height // 2, height, start_a, 0)

    blocks[zero_block] = jnp.zeros((tile, tile), jnp.bfloat16)
    for running in (running_even, running_odd):
        running[pairs] = jnp.zeros((tile, tile), jnp.float32)

    def clear(c, carry):
        for r in range(CB):
            out_ref[r, c] = jnp.zeros((tile, tile), jnp.float32)
        return carry

    lax.fori_loop(0, column_count, clear, 0)

    for side in range(2):
        for copy in ghost_copies(side):
            copy.wait_recv()
        for t in range(capacity):
            j = height + side * capacity + t
            blocks[j] = ghost_in[side, t]
            place = wrap(ghost_in_ids[side, t : t + 1] - start, coarse)
            group = group + jnp.where(listed == j, place_group(place), 0)

    lane = lax.broadcasted_iota(jnp.int32, listed.shape, 1)
    byte = jnp.where(group == 0, 1, jnp.where(group == 1, 1 << 8, 1 << 16))
    scan = jnp.where(lane < entries, byte, 0)
    step = 1
    while step < entries:
        scan = scan + jnp.where(lane >= step, pltpu.roll(scan, step, 1), 0)
        step *= 2
    total_counts = scan[:, entries - 1 : entries]
    counts = [(total_counts >> (8 * g)) & 255 for g in range(SPAN)]
    sizes = [((c + 1) >> 1) << 1 for c in counts]
    starts = [jnp.zeros_like(sizes[0]), sizes[0], sizes[0] + sizes[1]]
    slot = jnp.zeros_like(listed)
    for g in range(SPAN):
        slot = slot + jnp.where(group == g, starts[g] + ((scan >> (8 * g)) & 255) - 1, 0)
    packed = jnp.zeros_like(listed)
    for m in range(entries):
        packed = packed + jnp.where(
            slot[:, m : m + 1] == lane, (listed[:, m : m + 1] - zero_block) * 32 + m, 0
        )
    chosen = packed & 31
    column = (packed >> 5) + zero_block
    facts = jnp.ones_like(listed)
    for g in range(SPAN):
        facts = jnp.where(2 * lane == starts[g], 0, facts)
    for g in range(SPAN):
        last = jnp.where(counts[g] > 0, ((starts[g] + sizes[g]) >> 1) - 1, pairs)
        facts = jnp.where(lane == 16 + g, last, facts)
    table_v[...] = jnp.where(
        lane < 32,
        chosen,
        jnp.where(lane < 64, pltpu.roll(column, 32, 1), pltpu.roll(facts, 64, 1)),
    )
    table_copy = pltpu.make_async_copy(table_v, table, table_sem)
    table_copy.start()
    table_copy.wait()

    @pl.when(odd == 1)
    def _():
        send_slot(2)

    lax.fori_loop(0, height, wait_a, 0)

    def group_row(i, running):
        total = None
        for pair in range(pairs):
            at = (2 * pair, 2 * pair + 1)
            left = jnp.concatenate([a_buf[i, table[i, n]] for n in at], axis=1)
            right = jnp.concatenate([blocks[table[i, 32 + n]] for n in at], axis=0)
            term = jnp.dot(left, right, preferred_element_type=jnp.float32)
            total = term if pair == 0 else jnp.where(table[i, 64 + pair] > 0, total, 0.0) + term
            running[pair] = total
        rows_of = pl.ds(pl.multiple_of(i * tile, tile), tile)
        for g in range(SPAN):
            grouped[rows_of, g * tile : (g + 1) * tile] = running[table[i, 80 + g]].astype(jnp.bfloat16)

    def multiply(both, carry):
        i = 2 * both
        group_row(i, running_even)
        group_row(i + 1, running_odd)

        @pl.when((odd == 0) & (i == height // 2))
        def _():
            forward_mark()
            forward(0)
            forward(1)

        @pl.when((odd == 0) & (i == height * 3 // 4))
        def _():
            forward(2)
            forward(3)

        return carry

    lax.fori_loop(0, height // 2, multiply, 0)

    own_column = first_column(s)

    def part_copy(side, o, wide):
        columns = pl.ds(SPAN - 1, 1) if wide else pl.ds(0, SPAN - 1)
        return pltpu.make_async_remote_copy(
            src_ref=part_out.at[side, o, columns],
            dst_ref=part_in.at[side, o, columns],
            send_sem=part_send.at[side, o, wide],
            recv_sem=part_recv.at[side, o, wide],
            device_id={"row": before if side == 0 else after},
            device_id_type=MESH,
        )

    @pl.when(odd == 1)
    def _():
        forward_mark()
        for part in range(PARTS - 1):
            forward(part)

    receive_slot(1)

    def use_slot(step, carry):
        second = lax.rem(step, 2)
        others = step == 2 * (1 - late) + second

        @pl.when(others & (odd + second == 1))
        def _():
            receive_slot(3)

        @pl.when(others & (odd == 1) & (second == 1))
        def _():
            forward(PARTS - 1)

        index = lax.rem(2 * late + 2 * (step // 2), 4) + odd + second - 2 * odd * second
        total = None
        for part in range(PARTS):
            left = slots[index, part]
            mark = jnp.concatenate(
                [marks[index, part * per_part + n : part * per_part + n + 1] for n in range(per_part)],
                axis=1,
            )
            high = (left.astype(jnp.float32) * mark).astype(jnp.bfloat16)
            left = jnp.concatenate([left - high, high], axis=0)
            depth = per_part * tile
            term = jnp.dot(
                left, grouped[part * depth : (part + 1) * depth], preferred_element_type=jnp.float32
            )
            total = term if total is None else total + term

        @pl.when(step < 2)
        def _():
            for g in range(SPAN):
                columns = slice(g * tile, (g + 1) * tile)
                part_out[0, second, g] = total[:tile, columns].astype(jnp.bfloat16)
                part_out[1, second, g] = total[tile:, columns].astype(jnp.bfloat16)
            for side in range(2):
                part_copy(side, second, 0).start()

            @pl.when(late == 1)
            def _():
                for side in range(2):
                    part_copy(side, second, 1).start()

        @pl.when(step >= 2)
        def _():
            for g in range(SPAN):
                out_ref[second, lax.rem(own_column + g, column_count)] = total[
                    :tile, g * tile : (g + 1) * tile
                ]

        return carry

    lax.fori_loop(0, 4, use_slot, 0)

    columns_in = [first_column(after), first_column(before)]

    def collect(o, carry):
        for side in range(2):

            def add(g):
                at = lax.rem(columns_in[side] + g, column_count)
                out_ref[o, at] = out_ref[o, at] + part_in[side, o, g].astype(jnp.float32)

            part_copy(side, o, 0).wait_recv()
            for g in range(SPAN - 1):
                add(g)

            @pl.when(late == 0)
            def _():
                part_copy(side, o, 1).wait_recv()
                add(SPAN - 1)

        return carry

    lax.fori_loop(0, CB, collect, 0)

    for side in range(2):
        for copy in ghost_copies(side):
            copy.wait_send()
        for o in range(CB):
            part_copy(side, o, 0).wait_send()

    @pl.when(late == 1)
    def _():
        for side in range(2):
            for o in range(CB):
                part_copy(side, o, 1).wait_send()

    for hop in (1, 2, 3):
        mark_copy(hop).wait_send()
        for part in range(PARTS):
            slot_copy(hop, part).wait_send()


def shards(a_tiles, a_cols, p_tiles, p_cols, send_rows):
    rows, cols = lax.axis_size("row"), lax.axis_size("col")
    assert cols == 4
    height, entries, tile, _ = a_tiles.shape
    capacity = send_rows.shape[1]
    column_count = CB * rows // cols
    width = SPAN * tile
    vmem = pl.BlockSpec(memory_space=pltpu.VMEM)
    operands = (a_cols, p_cols.reshape(height), send_rows, p_tiles, a_tiles)
    bf16, f32, i32 = jnp.bfloat16, jnp.float32, jnp.int32
    dma = pltpu.SemaphoreType.DMA
    return pl.pallas_call(
        functools.partial(kernel, rows),
        out_shape=jax.ShapeDtypeStruct((CB, column_count, tile, tile), f32),
        in_specs=[pl.BlockSpec(memory_space=pltpu.HBM)] * 5,
        out_specs=vmem,
        scratch_shapes=[
            pltpu.VMEM(a_cols.shape, i32),
            pltpu.SMEM((height,), i32),
            pltpu.SMEM(send_rows.shape, i32),
            pltpu.VMEM(p_tiles.shape, bf16),
            pltpu.VMEM(a_tiles.shape, bf16),
            pltpu.VMEM((2, capacity, tile, tile), bf16),
            pltpu.VMEM((2, 8, tile), i32),
            pltpu.VMEM((2, capacity, tile, tile), bf16),
            pltpu.VMEM((2, 8, tile), i32),
            pltpu.VMEM((4, PARTS, tile, height // PARTS * tile), bf16),
            pltpu.VMEM((4, height, tile), f32),
            pltpu.VMEM((height + 2 * capacity + 1, tile, tile), bf16),
            pltpu.VMEM(((entries + SPAN) // 2 + 1, tile, tile), f32),
            pltpu.VMEM(((entries + SPAN) // 2 + 1, tile, tile), f32),
            pltpu.VMEM((height, 128), i32),
            pltpu.VMEM((height, 128), i32),
            pltpu.SMEM((height, 128), i32),
            pltpu.VMEM((height * tile, width), bf16),
            pltpu.VMEM((2, CB, SPAN, tile, tile), bf16),
            pltpu.VMEM((2, CB, SPAN, tile, tile), bf16),
            dma((4,)),
            dma,
            dma((height,)),
            dma((2, 2)),
            dma((2, 2)),
            dma((3, PARTS)),
            dma((3, PARTS)),
            dma((3,)),
            dma((3,)),
            dma((2, CB, 2)),
            dma((2, CB, 2)),
        ],
        compiler_params=pltpu.CompilerParams(
            collective_id=0, has_side_effects=True, vmem_limit_bytes=48 * 1024 * 1024
        ),
        cost_estimate=pl.CostEstimate(
            flops=2 * height * entries * tile * tile * width,
            bytes_accessed=2 * a_tiles.size,
            transcendentals=0,
        ),
    )(*(pltpu.with_memory_space_constraint(x, pltpu.HBM) for x in operands))


def solution(mesh):
    in_specs = (
        P("row", None, None, None),
        P("row", None),
        P("row", "col", None, None),
        P("row", "col"),
        P("row", None),
    )
    out_specs = P("row", "col", None, None)
    return jax.shard_map(shards, mesh=mesh, in_specs=in_specs, out_specs=out_specs, check_vma=False)
```
